32 devices in a mesh: design: 2 (over y), leaf: 4 (over z), vec: 2 (over x), sub: 2 (over core).
Axes of the slice: x: 2, y: 2, z: 4, core: 2. Of those that a mesh axis runs over, the one named last changes fastest.
Arguments:
- adjoint: bfloat16 [64, 32, 256], P(('design', 'leaf', 'vec'), 'sub'), parts along dimension 0, may hold values from -6 to 6
- leaf_basis_out: bfloat16 [64, 64, 256], P(('design', 'leaf', 'vec')), parts along dimension 0, may hold values from -0.375 to 0.375
- leaf_basis_in: bfloat16 [64, 64, 256], P(('design', 'leaf', 'vec')), parts along dimension 0, may hold values from -0.75 to 0.75
- transfer_up: bfloat16 [16, 64, 256], P(('design', 'leaf', 'vec')), parts along dimension 0, may hold values from -0.375 to 0.375
- transfer_down: bfloat16 [16, 64, 256], P(('design', 'leaf', 'vec')), parts along dimension 0, may hold values from -0.75 to 0.75
- far_coupling: bfloat16 [64, 64, 512], P(('design', 'leaf', 'vec')), parts along dimension 0, may hold values from -0.25 to 0.25
- top_coupling: bfloat16 [16, 64, 1024], P(('design', 'leaf', 'vec')), parts along dimension 0, may hold values from -0.1875 to 0.1875
- near_tiles: bfloat16 [64, 768, 256], P(('design', 'leaf', 'vec')), parts along dimension 0, may hold values from -0.21875 to 0.21875
- near_src: int32 [64, 3], P(('design', 'leaf', 'vec')), parts along dimension 0, may hold values from 0 to 31, as said below
- far_dst: int32 [64, 8], P(('design', 'leaf', 'vec')), parts along dimension 0, may hold values from 0 to 31, as said below
- top_src: int32 [16, 16], P(('design', 'leaf', 'vec')), parts along dimension 0, may hold values from 0 to 7, as said below
Outputs:
- response: float32 [64, 32, 256], P(('design', 'leaf', 'vec'), 'sub'), parts along dimension 0
The draws below stay inside these ranges and needn't reach their ends.
There are 2 independent parts, one for each index of `design`. The reference program is written for one: setup_inputs(seed, part) draws one part's arguments, and reference() takes and returns one part's arrays. A program takes and returns all parts, laid end to end along the dimension named above; each array names one. Nothing has to cross between parts.
Inputs may be any that keep to these rules, and one draw needn't show every extreme that they name: `near_src`: entry 0 of row j is j itself; the other entries lie in j's aligned block of 4 leaves or in the aligned blocks just before and after it. `far_dst`: entry [i, k] lies in an aligned block of 4 leaves that is 1 to 4 blocks away from i's block. The targets that the rows of one block name within any one other block are at most 2 distinct leaves; every block reaches 2 in some other block. `top_src`: entry [D, k] differs from D by 1 to 8 - 1 modulo 8; entry [D, 0] is D - 1 modulo 8.
All inputs are finite; a program needn't handle non-finite values.
Results may differ from the reference program's by a relative error of at most 0.0042.
Values may be sent and summed in bfloat16 or wider, within the bound.
No kernel may reach another device: no remote copies, remote signals or barrier semaphores. Data moves between devices by JAX's collectives and lax.ppermute only.
A program may use at most 64 MiB of HBM per device.

```python
import jax
import jax.numpy as jnp

LS = 256
R = 64
LEAF_DEV = 4
NEAR = 3
FAR = 8
FART = 16
CAP = 2
NODES = 8
LEAVES = 32
NV = 32


def draw_near_src(key, part):
    key = jax.random.fold_in(key, 11)
    target = jnp.arange(LEAVES, dtype=jnp.int32)[:, None]
    start = target // LEAF_DEV * LEAF_DEV
    offset = jax.random.randint(key, (LEAVES, NEAR), -LEAF_DEV, 2 * LEAF_DEV, dtype=jnp.int32)
    source = start + offset
    inside = (source >= 0) & (source < LEAVES)
    source = jnp.where(inside, source, start + offset % LEAF_DEV)
    column = jnp.arange(NEAR, dtype=jnp.int32)[None, :]
    return jnp.where(column == 0, target, source).astype(jnp.int32)


def draw_far_dst(key, part):
    key = jax.random.fold_in(key, 23)
    keys = jax.random.split(key, 5)
    entries = LEAF_DEV * FAR
    window = min(5, NODES // 2)
    node = jnp.arange(NODES, dtype=jnp.int32)[:, None]
    entry = jnp.arange(entries, dtype=jnp.int32)[None, :]
    first_draw = jax.random.randint(keys[0], (NODES, entries), 0, window, dtype=jnp.int32)
    second_draw = jax.random.randint(keys[1], (NODES, entries), 0, window, dtype=jnp.int32)
    offset = 1 + jnp.minimum(first_draw, second_draw)
    upward = jax.random.randint(keys[2], (NODES, entries), 0, 2, dtype=jnp.int32)
    above = node + offset
    below = node - offset
    dest = jnp.where(upward == 1, jnp.where(above < NODES, above, below), jnp.where(below >= 0, below, above))
    before = jnp.where(node >= 1, node - 1, node + 1)
    dest = jnp.where(entry == 0, before, dest)
    dest = jnp.where(entry < CAP, dest[:, :1], dest)
    which = jax.random.randint(keys[3], (NODES, entries), 0, CAP, dtype=jnp.int32)
    which = jnp.where(entry < CAP, entry, which)
    anchor = jax.random.randint(keys[4], (NODES, NODES), 0, LEAF_DEV, dtype=jnp.int32)
    base = jnp.take_along_axis(anchor, dest, axis=1)
    target = dest * LEAF_DEV + (base + which) % LEAF_DEV
    return target.reshape(LEAVES, FAR).astype(jnp.int32)


def draw_top_src(key, part):
    key = jax.random.fold_in(key, 37)
    offset = jax.random.randint(key, (NODES, FART), 1, NODES, dtype=jnp.int32)
    column = jnp.arange(FART, dtype=jnp.int32)[None, :]
    offset = jnp.where(column == 0, NODES - 1, offset)
    node = jnp.arange(NODES, dtype=jnp.int32)[:, None]
    return ((node + offset) % NODES).astype(jnp.int32)


def levels(stream_key, extent, pieces, low, high):
    level, own = 1.0, jax.random.fold_in(stream_key, 6)
    for dim, shards_of in pieces:
        heights = jnp.exp(jax.random.uniform(jax.random.fold_in(own, dim), (shards_of,), jnp.float32, low / len(pieces), high / len(pieces)))
        level = level * jnp.repeat(heights, extent[dim] // shards_of).reshape([-1 if axis == dim else 1 for axis in range(len(extent))])
    return level


def scatter_about(stream_key, extent, scale, most, cuts=(), held_as=jnp.bfloat16):
    result = scale * jax.random.normal(stream_key, extent, jnp.float32)
    if cuts:
        result = result * levels(stream_key, extent, cuts, -0.22, 0.18)
    return jnp.clip(result, -most, most).astype(held_as)


def setup_inputs(seed: int = 0, part: int = 0) -> dict:
    splits = jax.random.split(jax.random.key(seed), 12)
    part_keys = jax.random.split(jax.random.fold_in(splits[11], part), 12)
    adjoint = scatter_about(part_keys[0], (LEAVES, NV, LS), 1.0, 6.0, ((0, 8), (1, 2)))
    leaf_basis_out = scatter_about(part_keys[1], (LEAVES, R, LS), LS ** -0.5, 0.375, ((0, 8),))
    leaf_basis_in = scatter_about(part_keys[2], (LEAVES, R, LS), R ** -0.5, 0.75, ((0, 8),))
    transfer_up = scatter_about(part_keys[3], (NODES, R, LEAF_DEV * R), (R * LEAF_DEV) ** -0.5, 0.375, ((0, 8),))
    transfer_down = scatter_about(part_keys[4], (NODES, R, LEAF_DEV * R), R ** -0.5, 0.75, ((0, 8),))
    far_coupling = scatter_about(part_keys[5], (LEAVES, R, FAR * R), (R * FAR) ** -0.5, 0.25, ((0, 8),))
    top_coupling = scatter_about(part_keys[6], (NODES, R, FART * R), (R * FART) ** -0.5, 0.1875, ((0, 8),))
    near_tiles = scatter_about(part_keys[7], (LEAVES, NEAR * LS, LS), (LS * NEAR) ** -0.5, 0.21875, ((0, 8),))
    near_src = draw_near_src(jax.random.fold_in(jax.random.fold_in(splits[11], part), 71), part)
    far_dst = draw_far_dst(jax.random.fold_in(jax.random.fold_in(splits[11], part), 71), part)
    top_src = draw_top_src(jax.random.fold_in(jax.random.fold_in(splits[11], part), 71), part)
    return dict(adjoint=adjoint, leaf_basis_out=leaf_basis_out, leaf_basis_in=leaf_basis_in, transfer_up=transfer_up, transfer_down=transfer_down, far_coupling=far_coupling, top_coupling=top_coupling, near_tiles=near_tiles, near_src=near_src, far_dst=far_dst, top_src=top_src)


def reference(adjoint, leaf_basis_out, leaf_basis_in, transfer_up, transfer_down, far_coupling, top_coupling, near_tiles, near_src, far_dst, top_src):
    f32 = jnp.float32
    bf16 = jnp.bfloat16
    leaf_coef = jnp.einsum('jvc,jrc->jvr', adjoint.astype(f32), leaf_basis_out.astype(f32)).astype(bf16)
    side = leaf_coef.reshape(NODES, LEAF_DEV, NV, R).transpose(0, 2, 1, 3).reshape(NODES, NV, LEAF_DEV * R)
    node_coef = jnp.einsum('dvm,drm->dvr', side.astype(f32), transfer_up.astype(f32)).astype(bf16)
    picked = node_coef[top_src].transpose(0, 2, 1, 3).reshape(NODES, NV, FART * R)
    top_in = jnp.einsum('dvm,drm->dvr', picked.astype(f32), top_coupling.astype(f32)).astype(bf16)
    down = jnp.einsum('dvr,drm->dvm', top_in.astype(f32), transfer_down.astype(f32))
    down = down.reshape(NODES, NV, LEAF_DEV, R).transpose(0, 2, 1, 3).reshape(LEAVES, NV, R)
    contrib = jnp.einsum('ivr,irm->ivm', leaf_coef.astype(f32), far_coupling.astype(f32))
    contrib = contrib.reshape(LEAVES, NV, FAR, R).transpose(0, 2, 1, 3).reshape(LEAVES * FAR, NV * R)
    leaf_in = jax.ops.segment_sum(contrib, far_dst.reshape(-1), num_segments=LEAVES).reshape(LEAVES, NV, R)
    mixed = (leaf_in + down).astype(bf16)
    far_out = jnp.einsum('jvr,jrc->jvc', mixed.astype(f32), leaf_basis_in.astype(f32))
    gathered = adjoint[near_src].astype(f32)
    tiles = near_tiles.reshape(LEAVES, NEAR, LS, LS).astype(f32)
    near_out = jnp.einsum('jkvc,jkcd->jvd', gathered, tiles)
    return far_out + near_out
```

```python
import functools

import jax
import jax.numpy as jnp
from jax import lax
from jax.experimental import pallas as pl
from jax.experimental.pallas import tpu as pltpu
from jax.sharding import PartitionSpec as P

F32 = jnp.float32
BF16 = jnp.bfloat16
NODE_AXES = ("leaf", "vec")
NT = (((1,), (1,)), ((), ()))


def bits_of(count):
    return count.bit_length() - 1


def reversed_bits(value, width):
    return sum(((value >> bit) & 1) << (width - 1 - bit) for bit in range(width))


def lane_half(shape):
    return lax.broadcasted_iota(jnp.int32, shape, 1) // (shape[1] // 2)


def source_kernel(nodes, me_ref, dst_ref, adj_ref, out_ref, up_ref, far_ref, send_ref, keep_ref, sums):
    leaf_dev, vectors, _ = adj_ref.shape
    rank = out_ref.shape[1]
    far_count = dst_ref.shape[1]
    pairs = leaf_dev // 2
    wide = 2 * rank
    me = me_ref[0]
    sums[...] = jnp.zeros_like(sums)
    half = lane_half((vectors, wide))
    coefs = []
    for j in range(leaf_dev):
        coef = lax.dot_general(adj_ref[j], out_ref[j], NT, preferred_element_type=F32).astype(BF16)
        coefs.append(coef)
        contrib = jnp.dot(coef, far_ref[j], preferred_element_type=F32)
        for g in range(far_count // 2):
            straight = contrib[:, g * wide : (g + 1) * wide]
            turned = pltpu.roll(straight, rank, 1)
            for h in range(2):
                target = dst_ref[j, 2 * g + h]
                place = ((target // leaf_dev) ^ me) * pairs + (target % leaf_dev) // 2
                side = target % 2
                value = jnp.where(jnp.full(half.shape, side) == h, straight, turned)
                sums[place] += jnp.where(half == side, value, 0.0)
    side = jnp.concatenate(coefs, axis=1)
    node = lax.dot_general(side, up_ref[0], NT, preferred_element_type=F32).astype(BF16)
    rows = pairs * vectors
    width = bits_of(nodes)
    for r in range(nodes):
        d = reversed_bits(r, width)
        block = sums[d * pairs : (d + 1) * pairs].reshape(rows, wide)
        if r < nodes // 2:
            keep_ref[r * rows : (r + 1) * rows] = block
        else:
            at = (r - nodes // 2) * rows
            send_ref[at : at + rows] = block.astype(BF16)
    send_ref[nodes // 2 * rows :] = jnp.concatenate([node, node], axis=1)


def near_kernel(me_ref, src_ref, adj_ref, a_ref, b_ref, tiles_ref, near_ref, around):
    leaf_dev, _, cells = adj_ref.shape
    near_count = src_ref.shape[1]
    me = me_ref[0]
    around[:leaf_dev] = adj_ref[...]
    around[leaf_dev : 2 * leaf_dev] = a_ref[...]
    around[2 * leaf_dev :] = b_ref[...]
    for j in range(leaf_dev):
        total = None
        for k in range(near_count):
            source = src_ref[j, k]
            node = source // leaf_dev
            base = jnp.where(node == me, 0, jnp.where(node == (me ^ 1), leaf_dev, 2 * leaf_dev))
            block = around[base + source % leaf_dev]
            part = jnp.dot(block, tiles_ref[j, k * cells : (k + 1) * cells], preferred_element_type=F32)
            total = part if total is None else total + part
        near_ref[j] = total


def final_kernel(me_ref, src_ref, keep_ref, got_ref, *refs):
    *coef_refs, top_ref, down_ref, in_ref, near_ref, out_ref, held = refs
    leaf_dev, vectors, cells = near_ref.shape
    rank = in_ref.shape[1]
    wide = 2 * rank
    me = me_ref[0]
    at = 0
    for ref in coef_refs:
        count = ref.shape[0] // vectors
        held[at : at + count] = ref[...].astype(F32).reshape(count, vectors, wide)
        at += count
    half = lane_half((vectors, wide))
    top_count = src_ref.shape[1]
    picked = []
    for q in range(top_count // 2):
        sides = []
        for h in range(2):
            distance = src_ref[0, 2 * q + h] ^ me
            block = held[distance // 2]
            turned = pltpu.roll(block, rank, 1)
            sides.append(jnp.where(jnp.full(half.shape, distance % 2) == h, block, turned))
        picked.append(jnp.where(half == 0, sides[0], sides[1]).astype(BF16))
    picked = jnp.concatenate(picked, axis=1)
    top_in = lax.dot_general(picked, top_ref[0], NT, preferred_element_type=F32).astype(BF16)
    down = jnp.dot(top_in, down_ref[0], preferred_element_type=F32)
    leaf_in = keep_ref[...] + got_ref[...].astype(F32)
    leaf_in = jnp.concatenate([leaf_in[p * vectors : (p + 1) * vectors] for p in range(leaf_dev // 2)], axis=1)
    mixed = (leaf_in + down).astype(BF16)
    for j in range(leaf_dev):
        far = jnp.dot(mixed[:, j * rank : (j + 1) * rank], in_ref[j], preferred_element_type=F32)
        out_ref[j] = near_ref[j] + far


VMEM = pl.BlockSpec(memory_space=pltpu.VMEM)
SMEM = pl.BlockSpec(memory_space=pltpu.SMEM)


def on_device(
    adjoint, leaf_basis_out, leaf_basis_in, transfer_up, transfer_down, far_coupling, top_coupling, near_tiles, near_src, far_dst, top_src
):
    leaf_dev, vectors, cells = adjoint.shape
    rank = leaf_basis_out.shape[1]
    wide = 2 * rank
    pairs = leaf_dev // 2
    rows = pairs * vectors
    nodes = lax.axis_size(NODE_AXES)
    steps = bits_of(nodes)
    me = lax.axis_index(NODE_AXES).astype(jnp.int32).reshape(1)

    def exchange(x, distance):
        return lax.ppermute(x, NODE_AXES, [(i, i ^ distance) for i in range(nodes)])

    send, keep = pl.pallas_call(
        functools.partial(source_kernel, nodes),
        out_shape=(
            jax.ShapeDtypeStruct((nodes // 2 * rows + vectors, wide), BF16),
            jax.ShapeDtypeStruct((nodes // 2 * rows, wide), F32),
        ),
        in_specs=[SMEM, SMEM] + [VMEM] * 4,
        out_specs=(VMEM, VMEM),
        scratch_shapes=[pltpu.VMEM((nodes * pairs, vectors, wide), F32)],
        name="source",
    )(me, far_dst, adjoint, leaf_basis_out, transfer_up, far_coupling)

    other = [pair for i in range(1, nodes - 1, 2) for pair in ((i, i + 1), (i + 1, i))]
    a = exchange(adjoint, 1)
    b = lax.ppermute(adjoint, NODE_AXES, other)

    coefs = [send[nodes // 2 * rows :]]
    for step in range(steps):
        got = exchange(send, 1 << step)
        half = nodes >> (step + 1)
        arrived = got[half * rows :]
        if step == 0:
            left = jnp.arange(wide) < rank
            coefs = [jnp.where(left, coefs[0], arrived)]
        else:
            coefs.append(arrived)
        if step < steps - 1:
            keep = keep + got[: half * rows].astype(F32)
            send = jnp.concatenate([keep[half // 2 * rows :].astype(BF16)] + coefs, axis=0)
            keep = keep[: half // 2 * rows]

    near = pl.pallas_call(
        near_kernel,
        out_shape=jax.ShapeDtypeStruct((leaf_dev, vectors, cells), F32),
        in_specs=[SMEM, SMEM] + [VMEM] * 4,
        out_specs=VMEM,
        scratch_shapes=[pltpu.VMEM((3 * leaf_dev, vectors, cells), BF16)],
        name="near",
    )(me, near_src, adjoint, a, b, near_tiles)

    return pl.pallas_call(
        final_kernel,
        out_shape=jax.ShapeDtypeStruct((leaf_dev, vectors, cells), F32),
        in_specs=[SMEM, SMEM] + [VMEM] * (6 + len(coefs)),
        out_specs=VMEM,
        scratch_shapes=[pltpu.VMEM((nodes // 2, vectors, wide), F32)],
        name="final",
    )(me, top_src, keep, got[:rows], *coefs, top_coupling, transfer_down, leaf_basis_in, near)


def solution(mesh):
    split = P(("design", "leaf", "vec"), None, None)
    in_specs = (P(("design", "leaf", "vec"), "sub", None),) + (split,) * 7 + (P(("design", "leaf", "vec"), None),) * 3
    out_specs = P(("design", "leaf", "vec"), "sub", None)
    return jax.shard_map(on_device, mesh=mesh, in_specs=in_specs, out_specs=out_specs, check_vma=False)
```

```python
import functools

import jax
import jax.numpy as jnp
from jax import lax
from jax.experimental import pallas as pl
from jax.experimental.pallas import tpu as pltpu
from jax.sharding import PartitionSpec as P

F32 = jnp.float32
BF16 = jnp.bfloat16
NODE_AXES = ("leaf", "vec")
NT = (((1,), (1,)), ((), ()))
TN = (((0,), (0,)), ((), ()))
VMEM = pl.BlockSpec(memory_space=pltpu.VMEM)
HBM = pl.BlockSpec(memory_space=pltpu.HBM)
PARAMS = pltpu.CompilerParams(vmem_limit_bytes=24 << 20)


def bits_of(count):
    return count.bit_length() - 1


def reversed_bits(value, width):
    return sum(((value >> bit) & 1) << (width - 1 - bit) for bit in range(width))


def lane_half(shape):
    return lax.broadcasted_iota(jnp.int32, shape, 1) // (shape[1] // 2)


def in_hbm(x):
    return pltpu.with_memory_space_constraint(x, pltpu.HBM)


def side_by_side(stacked, rows):
    return jnp.concatenate([stacked[at : at + rows] for at in range(0, stacked.shape[0], rows)], axis=1)


def source_kernel(nodes, *refs):
    inputs, rest = refs[:9], refs[9:]
    dst_hbm, adj_hbm, out_hbm, up_hbm, far_hbm = inputs[:5]
    send_ref, keep_ref, adj_ref = rest[:3]
    later = rest[3:7]
    dst_ref, out_ref, up_ref, far_ref, sums, sems = rest[7:]
    pairs_of_refs = [(dst_hbm, dst_ref), (adj_hbm, adj_ref), (out_hbm, out_ref), (far_hbm, far_ref), (up_hbm, up_ref)]
    pairs_of_refs += list(zip(inputs[5:], later))
    copies = [pltpu.make_async_copy(a, b, sems.at[i]) for i, (a, b) in enumerate(pairs_of_refs)]
    for copy in copies:
        copy.start()
    leaf_dev, vectors, _ = adj_ref.shape
    rank = out_ref.shape[1]
    far_count = dst_ref.shape[1]
    pairs = leaf_dev // 2
    wide = 2 * rank
    me = lax.axis_index(NODE_AXES)
    sums[...] = jnp.zeros_like(sums)
    half = lane_half((vectors, wide))
    for copy in copies[:4]:
        copy.wait()
    coefs = []
    for j in range(leaf_dev):
        coef = lax.dot_general(adj_ref[j], out_ref[j], NT, preferred_element_type=F32).astype(BF16)
        coefs.append(coef)
        contrib = jnp.dot(coef, far_ref[j], preferred_element_type=F32)
        for g in range(far_count // 2):
            straight = contrib[:, g * wide : (g + 1) * wide]
            turned = pltpu.roll(straight, rank, 1)
            for h in range(2):
                target = dst_ref[j, 2 * g + h]
                place = ((target // leaf_dev) ^ me) * pairs + (target % leaf_dev) // 2
                side = target % 2
                value = jnp.where(jnp.full(half.shape, side) == h, straight, turned)
                sums[place] += jnp.where(half == side, value, 0.0)
    copies[4].wait()
    side = jnp.concatenate(coefs, axis=1)
    node = lax.dot_general(side, up_ref[0], NT, preferred_element_type=F32).astype(BF16)
    rows = pairs * vectors
    width = bits_of(nodes)
    for r in range(nodes):
        d = reversed_bits(r, width)
        block = sums[d * pairs : (d + 1) * pairs].reshape(rows, wide)
        if r < nodes // 2:
            keep_ref[r * rows : (r + 1) * rows] = block
        else:
            at = (r - nodes // 2) * rows
            send_ref[at : at + rows] = block.astype(BF16)
    send_ref[nodes // 2 * rows :] = jnp.concatenate([node, node], axis=1)
    for copy in copies[5:]:
        copy.wait()


def near_kernel(nodes, near_hbm, top_hbm, adj_ref, a_ref, b_ref, tiles_ref, top_ref, down_ref, keep_ref, *refs):
    *coef_refs, near_ref, base_ref, rest_ref, near_src, top_src, around, by_node, sems = refs
    copies = [pltpu.make_async_copy(top_hbm, top_src, sems.at[0]), pltpu.make_async_copy(near_hbm, near_src, sems.at[1])]
    for copy in copies:
        copy.start()
    leaf_dev, vectors, cells = adj_ref.shape
    near_count = near_src.shape[1]
    top_count = top_src.shape[1]
    rank = down_ref.shape[1]
    me = lax.axis_index(NODE_AXES)
    around[:leaf_dev] = adj_ref[...]
    around[leaf_dev : 2 * leaf_dev] = a_ref[...]
    around[2 * leaf_dev :] = b_ref[...]
    by_node[...] = jnp.zeros_like(by_node)
    through = lax.dot_general(top_ref[0], down_ref[0], TN, preferred_element_type=F32)
    copies[0].wait()
    for k in range(top_count):
        by_node[top_src[0, k] ^ me] += through[k * rank : (k + 1) * rank]
    copies[1].wait()
    for j in range(leaf_dev):
        total = None
        for k in range(near_count):
            source = near_src[j, k]
            node = source // leaf_dev
            base = jnp.where(node == me, 0, jnp.where(node == (me ^ 1), leaf_dev, 2 * leaf_dev))
            block = around[base + source % leaf_dev]
            part = jnp.dot(block, tiles_ref[j, k * cells : (k + 1) * cells], preferred_element_type=F32)
            total = part if total is None else total + part
        near_ref[j] = total
    known = nodes // 2
    at = 0
    base = side_by_side(keep_ref[...], vectors)
    for ref in coef_refs:
        count = 2 * ref.shape[0] // vectors
        matrix = by_node[at : at + count].reshape(count * rank, leaf_dev * rank).astype(BF16)
        base = base + jnp.dot(side_by_side(ref[...], vectors), matrix, preferred_element_type=F32)
        at += count
    base_ref[...] = base
    rest_ref[...] = by_node[known:].reshape(known * rank, leaf_dev * rank).astype(BF16)


def final_kernel(got_ref, base_ref, rest_ref, in_ref, near_ref, out_ref):
    leaf_dev, vectors, _ = near_ref.shape
    rank = in_ref.shape[1]
    rows = leaf_dev // 2 * vectors
    got = got_ref[...]
    down = jnp.dot(side_by_side(got[rows:], vectors), rest_ref[...], preferred_element_type=F32)
    mixed = (base_ref[...] + side_by_side(got[:rows].astype(F32), vectors) + down).astype(BF16)
    for j in range(leaf_dev):
        far = jnp.dot(mixed[:, j * rank : (j + 1) * rank], in_ref[j], preferred_element_type=F32)
        out_ref[j] = near_ref[j] + far


def on_device(
    adjoint, leaf_basis_out, leaf_basis_in, transfer_up, transfer_down, far_coupling, top_coupling, near_tiles, near_src, far_dst, top_src
):
    leaf_dev, vectors, cells = adjoint.shape
    rank = leaf_basis_out.shape[1]
    wide = 2 * rank
    pairs = leaf_dev // 2
    rows = pairs * vectors
    nodes = lax.axis_size(NODE_AXES)
    steps = bits_of(nodes)

    def exchange(x, distance):
        return lax.ppermute(x, NODE_AXES, [(i, i ^ distance) for i in range(nodes)])

    def like(x):
        return jax.ShapeDtypeStruct(x.shape, x.dtype)

    later = (near_tiles, top_coupling, transfer_down, leaf_basis_in)
    send, keep, adjoint_v, tiles, top, down, basis_in = pl.pallas_call(
        functools.partial(source_kernel, nodes),
        out_shape=(
            jax.ShapeDtypeStruct((nodes // 2 * rows + vectors, wide), BF16),
            jax.ShapeDtypeStruct((nodes // 2 * rows, wide), F32),
            like(adjoint),
            *map(like, later),
        ),
        in_specs=[HBM] * 9,
        out_specs=(VMEM,) * 7,
        scratch_shapes=[
            pltpu.SMEM(far_dst.shape, jnp.int32),
            pltpu.VMEM(leaf_basis_out.shape, BF16),
            pltpu.VMEM(transfer_up.shape, BF16),
            pltpu.VMEM(far_coupling.shape, BF16),
            pltpu.VMEM((nodes * pairs, vectors, wide), F32),
            pltpu.SemaphoreType.DMA((9,)),
        ],
        compiler_params=PARAMS,
        name="source",
    )(*map(in_hbm, (far_dst, adjoint, leaf_basis_out, transfer_up, far_coupling, *later)))

    other = [(i, (i + (1 if i % 2 else -1)) % nodes) for i in range(nodes)]
    a = exchange(adjoint_v, 1)
    b = lax.ppermute(adjoint_v, NODE_AXES, other)

    coefs = [send[nodes // 2 * rows :]]
    for step in range(steps):
        got = exchange(send, 1 << step)
        half = nodes >> (step + 1)
        if step < steps - 1:
            arrived = got[half * rows :]
            if step == 0:
                left = jnp.arange(wide) < rank
                coefs = [jnp.where(left, coefs[0], arrived)]
            else:
                coefs.append(arrived)
            keep = keep + got[: half * rows].astype(F32)
            send = jnp.concatenate([keep[half // 2 * rows :].astype(BF16)] + coefs, axis=0)
            keep = keep[: half // 2 * rows]

    near, base, rest = pl.pallas_call(
        functools.partial(near_kernel, nodes),
        out_shape=(
            jax.ShapeDtypeStruct((leaf_dev, vectors, cells), F32),
            jax.ShapeDtypeStruct((vectors, leaf_dev * rank), F32),
            jax.ShapeDtypeStruct((nodes // 2 * rank, leaf_dev * rank), BF16),
        ),
        in_specs=[HBM] * 2 + [VMEM] * (7 + len(coefs)),
        out_specs=(VMEM,) * 3,
        scratch_shapes=[
            pltpu.SMEM(near_src.shape, jnp.int32),
            pltpu.SMEM(top_src.shape, jnp.int32),
            pltpu.VMEM((3 * leaf_dev, vectors, cells), BF16),
            pltpu.VMEM((nodes, rank, leaf_dev * rank), F32),
            pltpu.SemaphoreType.DMA((2,)),
        ],
        compiler_params=PARAMS,
        name="near",
    )(in_hbm(near_src), in_hbm(top_src), adjoint_v, a, b, tiles, top, down, keep, *coefs)

    return pl.pallas_call(
        final_kernel,
        out_shape=jax.ShapeDtypeStruct((leaf_dev, vectors, cells), F32),
        in_specs=[VMEM] * 5,
        out_specs=VMEM,
        compiler_params=PARAMS,
        name="final",
    )(got, base, rest, basis_in, near)


def solution(mesh):
    split = P(("design", "leaf", "vec"), None, None)
    in_specs = (P(("design", "leaf", "vec"), "sub", None),) + (split,) * 7 + (P(("design", "leaf", "vec"), None),) * 3
    out_specs = P(("design", "leaf", "vec"), "sub", None)
    return jax.shard_map(on_device, mesh=mesh, in_specs=in_specs, out_specs=out_specs, check_vma=False)
```

```python
import functools

import jax
import jax.numpy as jnp
from jax import lax
from jax.experimental import pallas as pl
from jax.experimental.pallas import tpu as pltpu
from jax.sharding import PartitionSpec as P

F32 = jnp.float32
BF16 = jnp.bfloat16
NODE_AXES = ("leaf", "vec")
NT = (((1,), (1,)), ((), ()))
TN = (((0,), (0,)), ((), ()))
VMEM = pl.BlockSpec(memory_space=pltpu.VMEM)
HBM = pl.BlockSpec(memory_space=pltpu.HBM)
PARAMS = pltpu.CompilerParams(vmem_limit_bytes=24 << 20)


def bits_of(count):
    return count.bit_length() - 1


def reversed_bits(value, width):
    return sum(((value >> bit) & 1) << (width - 1 - bit) for bit in range(width))


def lane_half(shape):
    return lax.broadcasted_iota(jnp.int32, shape, 1) // (shape[1] // 2)


def in_hbm(x):
    return pltpu.with_memory_space_constraint(x, pltpu.HBM)


def side_by_side(stacked, rows):
    return jnp.concatenate([stacked[at : at + rows] for at in range(0, stacked.shape[0], rows)], axis=1)


def source_kernel(nodes, *refs):
    inputs, rest = refs[:9], refs[9:]
    dst_hbm, adj_hbm, out_hbm, up_hbm, far_hbm = inputs[:5]
    send_ref, keep_ref, adj_ref = rest[:3]
    later = rest[3:7]
    dst_ref, out_ref, up_ref, far_ref, sums, sems = rest[7:]
    pairs_of_refs = [(dst_hbm, dst_ref), (adj_hbm, adj_ref), (out_hbm, out_ref), (far_hbm, far_ref), (up_hbm, up_ref)]
    pairs_of_refs += list(zip(inputs[5:], later))
    copies = [pltpu.make_async_copy(a, b, sems.at[i]) for i, (a, b) in enumerate(pairs_of_refs)]
    for copy in copies:
        copy.start()
    leaf_dev, vectors, _ = adj_ref.shape
    rank = out_ref.shape[1]
    far_count = dst_ref.shape[1]
    pairs = leaf_dev // 2
    wide = 2 * rank
    me = lax.axis_index(NODE_AXES)
    sums[...] = jnp.zeros_like(sums)
    half = lane_half((vectors, wide))
    for copy in copies[:4]:
        copy.wait()
    coefs = []
    for j in range(leaf_dev):
        coef = lax.dot_general(adj_ref[j], out_ref[j], NT, preferred_element_type=F32).astype(BF16)
        coefs.append(coef)
        contrib = jnp.dot(coef, far_ref[j], preferred_element_type=F32)
        for g in range(far_count // 2):
            straight = contrib[:, g * wide : (g + 1) * wide]
            turned = pltpu.roll(straight, rank, 1)
            for h in range(2):
                target = dst_ref[j, 2 * g + h]
                place = ((target // leaf_dev) ^ me) * pairs + (target % leaf_dev) // 2
                side = target % 2
                value = jnp.where(jnp.full(half.shape, side) == h, straight, turned)
                sums[place] += jnp.where(half == side, value, 0.0)
    copies[4].wait()
    side = jnp.concatenate(coefs, axis=1)
    node = lax.dot_general(side, up_ref[0], NT, preferred_element_type=F32).astype(BF16)
    rows = pairs * vectors
    width = bits_of(nodes)
    for r in range(nodes):
        d = reversed_bits(r, width)
        block = sums[d * pairs : (d + 1) * pairs].reshape(rows, wide)
        if r < nodes // 2:
            keep_ref[r * rows : (r + 1) * rows] = block
        else:
            at = (r - nodes // 2) * rows
            send_ref[at : at + rows] = block.astype(BF16)
    send_ref[nodes // 2 * rows :] = jnp.concatenate([node, node], axis=1)
    for copy in copies[5:]:
        copy.wait()


def near_kernel(nodes, near_hbm, top_hbm, adj_ref, a_ref, b_ref, tiles_ref, top_ref, down_ref, keep_ref, *refs):
    *coef_refs, near_ref, base_ref, rest_ref, near_src, top_src, around, by_node, sems = refs
    copies = [pltpu.make_async_copy(top_hbm, top_src, sems.at[0]), pltpu.make_async_copy(near_hbm, near_src, sems.at[1])]
    for copy in copies:
        copy.start()
    leaf_dev, vectors, cells = adj_ref.shape
    near_count = near_src.shape[1]
    top_count = top_src.shape[1]
    rank = down_ref.shape[1]
    me = lax.axis_index(NODE_AXES)
    around[:leaf_dev] = adj_ref[...]
    around[leaf_dev : 2 * leaf_dev] = a_ref[...]
    around[2 * leaf_dev :] = b_ref[...]
    by_node[...] = jnp.zeros_like(by_node)
    through = lax.dot_general(top_ref[0], down_ref[0], TN, preferred_element_type=F32)
    copies[0].wait()
    for k in range(top_count):
        by_node[top_src[0, k] ^ me] += through[k * rank : (k + 1) * rank]
    copies[1].wait()
    for j in range(leaf_dev):
        total = None
        for k in range(near_count):
            source = near_src[j, k]
            node = source // leaf_dev
            base = jnp.where(node == me, 0, jnp.where(node == (me ^ 1), leaf_dev, 2 * leaf_dev))
            block = around[base + source % leaf_dev]
            part = jnp.dot(block, tiles_ref[j, k * cells : (k + 1) * cells], preferred_element_type=F32)
            total = part if total is None else total + part
        near_ref[j] = total
    known = nodes // 2
    at = 0
    base = side_by_side(keep_ref[...], vectors)
    for ref in coef_refs:
        count = 2 * ref.shape[0] // vectors
        matrix = by_node[at : at + count].reshape(count * rank, leaf_dev * rank).astype(BF16)
        base = base + jnp.dot(side_by_side(ref[...], vectors), matrix, preferred_element_type=F32)
        at += count
    base_ref[...] = base
    rest_ref[...] = by_node[known:].reshape(known * rank, leaf_dev * rank).astype(BF16)


def final_kernel(got_ref, base_ref, rest_ref, in_ref, near_ref, out_ref):
    leaf_dev, vectors, _ = near_ref.shape
    rank = in_ref.shape[1]
    rows = leaf_dev // 2 * vectors
    got = got_ref[...]
    down = jnp.dot(side_by_side(got[rows:], vectors), rest_ref[...], preferred_element_type=F32)
    mixed = (base_ref[...] + side_by_side(got[:rows].astype(F32), vectors) + down).astype(BF16)
    for j in range(leaf_dev):
        far = jnp.dot(mixed[:, j * rank : (j + 1) * rank], in_ref[j], preferred_element_type=F32)
        out_ref[j] = near_ref[j] + far


def on_device(
    adjoint, leaf_basis_out, leaf_basis_in, transfer_up, transfer_down, far_coupling, top_coupling, near_tiles, near_src, far_dst, top_src
):
    leaf_dev, vectors, cells = adjoint.shape
    rank = leaf_basis_out.shape[1]
    wide = 2 * rank
    pairs = leaf_dev // 2
    rows = pairs * vectors
    nodes = lax.axis_size(NODE_AXES)
    steps = bits_of(nodes)

    def exchange(x, distance):
        return lax.ppermute(x, NODE_AXES, [(i, i ^ distance) for i in range(nodes)])

    def like(x):
        return jax.ShapeDtypeStruct(x.shape, x.dtype)

    later = (near_tiles, top_coupling, transfer_down, leaf_basis_in)
    send, keep, adjoint_v, tiles, top, down, basis_in = pl.pallas_call(
        functools.partial(source_kernel, nodes),
        out_shape=(
            jax.ShapeDtypeStruct((nodes // 2 * rows + vectors, wide), BF16),
            jax.ShapeDtypeStruct((nodes // 2 * rows, wide), F32),
            like(adjoint),
            *map(like, later),
        ),
        in_specs=[HBM] * 9,
        out_specs=(VMEM,) * 7,
        scratch_shapes=[
            pltpu.SMEM(far_dst.shape, jnp.int32),
            pltpu.VMEM(leaf_basis_out.shape, BF16),
            pltpu.VMEM(transfer_up.shape, BF16),
            pltpu.VMEM(far_coupling.shape, BF16),
            pltpu.VMEM((nodes * pairs, vectors, wide), F32),
            pltpu.SemaphoreType.DMA((9,)),
        ],
        compiler_params=PARAMS,
        name="source",
    )(*map(in_hbm, (far_dst, adjoint, leaf_basis_out, transfer_up, far_coupling, *later)))

    cores = lax.axis_size("sub")
    inner = [(i, i + 1 if i % 2 else i - 1) for i in range(1, nodes - 1)]
    other = [(i * cores + c, j * cores + c) for i, j in inner for c in range(cores)]
    other += [(i * cores + c, i * cores + (c + 1) % cores) for i in (0, nodes - 1) for c in range(cores)]
    a = exchange(adjoint_v, 1)
    b = lax.ppermute(adjoint_v, NODE_AXES + ("sub",), other)

    coefs = [send[nodes // 2 * rows :]]
    for step in range(steps):
        got = exchange(send, 1 << step)
        half = nodes >> (step + 1)
        if step < steps - 1:
            arrived = got[half * rows :]
            if step == 0:
                left = jnp.arange(wide) < rank
                coefs = [jnp.where(left, coefs[0], arrived)]
            else:
                coefs.append(arrived)
            keep = keep + got[: half * rows].astype(F32)
            send = jnp.concatenate([keep[half // 2 * rows :].astype(BF16)] + coefs, axis=0)
            keep = keep[: half // 2 * rows]

    near, base, rest = pl.pallas_call(
        functools.partial(near_kernel, nodes),
        out_shape=(
            jax.ShapeDtypeStruct((leaf_dev, vectors, cells), F32),
            jax.ShapeDtypeStruct((vectors, leaf_dev * rank), F32),
            jax.ShapeDtypeStruct((nodes // 2 * rank, leaf_dev * rank), BF16),
        ),
        in_specs=[HBM] * 2 + [VMEM] * (7 + len(coefs)),
        out_specs=(VMEM,) * 3,
        scratch_shapes=[
            pltpu.SMEM(near_src.shape, jnp.int32),
            pltpu.SMEM(top_src.shape, jnp.int32),
            pltpu.VMEM((3 * leaf_dev, vectors, cells), BF16),
            pltpu.VMEM((nodes, rank, leaf_dev * rank), F32),
            pltpu.SemaphoreType.DMA((2,)),
        ],
        compiler_params=PARAMS,
        name="near",
    )(in_hbm(near_src), in_hbm(top_src), adjoint_v, a, b, tiles, top, down, keep, *coefs)

    return pl.pallas_call(
        final_kernel,
        out_shape=jax.ShapeDtypeStruct((leaf_dev, vectors, cells), F32),
        in_specs=[VMEM] * 5,
        out_specs=VMEM,
        compiler_params=PARAMS,
        name="final",
    )(got, base, rest, basis_in, near)


def solution(mesh):
    split = P(("design", "leaf", "vec"), None, None)
    in_specs = (P(("design", "leaf", "vec"), "sub", None),) + (split,) * 7 + (P(("design", "leaf", "vec"), None),) * 3
    out_specs = P(("design", "leaf", "vec"), "sub", None)
    return jax.shard_map(on_device, mesh=mesh, in_specs=in_specs, out_specs=out_specs, check_vma=False)
```

```python
import functools

import jax
import jax.numpy as jnp
from jax import lax
from jax.experimental import pallas as pl
from jax.experimental.pallas import tpu as pltpu
from jax.sharding import PartitionSpec as P

F32 = jnp.float32
BF16 = jnp.bfloat16
NODE_AXES = ("leaf", "vec")
NT = (((1,), (1,)), ((), ()))
TN = (((0,), (0,)), ((), ()))
VMEM = pl.BlockSpec(memory_space=pltpu.VMEM)
HBM = pl.BlockSpec(memory_space=pltpu.HBM)
PARAMS = pltpu.CompilerParams(vmem_limit_bytes=24 << 20)


def bits_of(count):
    return count.bit_length() - 1


def reversed_bits(value, width):
    return sum(((value >> bit) & 1) << (width - 1 - bit) for bit in range(width))


def lane_half(shape):
    return lax.broadcasted_iota(jnp.int32, shape, 1) // (shape[1] // 2)


def in_hbm(x):
    return pltpu.with_memory_space_constraint(x, pltpu.HBM)


def side_by_side(stacked, rows):
    return jnp.concatenate([stacked[at : at + rows] for at in range(0, stacked.shape[0], rows)], axis=1)


def source_kernel(nodes, *refs):
    sources, (send_ref, keep_ref, adj_ref, *later), scratch = refs[:9], refs[9:16], refs[16:]
    dst_ref, out_ref, far_ref, up_ref, sums, sems = scratch
    copies = [
        pltpu.make_async_copy(there, here, sems.at[i])
        for i, (there, here) in enumerate(zip(sources, (dst_ref, adj_ref, out_ref, far_ref, up_ref, *later)))
    ]
    for copy in copies:
        copy.start()
    leaf_dev, vectors, _ = adj_ref.shape
    rank = out_ref.shape[1]
    far_count = dst_ref.shape[1]
    pairs = leaf_dev // 2
    wide = 2 * rank
    within = bits_of(leaf_dev)
    me = lax.axis_index(NODE_AXES)
    sums[...] = jnp.zeros_like(sums)
    half = lane_half((vectors, wide))
    for copy in copies[:3]:
        copy.wait()
    coefs = [
        lax.dot_general(adj_ref[j], out_ref[j], NT, preferred_element_type=F32).astype(BF16) for j in range(leaf_dev)
    ]
    copies[3].wait()
    for j in range(leaf_dev):
        contrib = jnp.dot(coefs[j], far_ref[j], preferred_element_type=F32)
        for g in range(far_count // 2):
            straight = contrib[:, g * wide : (g + 1) * wide]
            turned = pltpu.roll(straight, rank, 1)
            for h in range(2):
                target = dst_ref[j, 2 * g + h]
                place = ((target >> within) ^ me) * pairs + ((target & (leaf_dev - 1)) >> 1)
                side = target & 1
                value = jnp.where(jnp.full(half.shape, side) == h, straight, turned)
                sums[j, place] += jnp.where(half == side, value, 0.0)
    copies[4].wait()
    node = lax.dot_general(jnp.concatenate(coefs, axis=1), up_ref[0], NT, preferred_element_type=F32).astype(BF16)
    node = jnp.concatenate([node, node], axis=1)
    rows = pairs * vectors
    width = bits_of(nodes)
    for r in range(nodes):
        d = reversed_bits(r, width)
        block = sum(sums[j, d * pairs : (d + 1) * pairs] for j in range(leaf_dev)).reshape(rows, wide)
        if r < nodes // 2:
            keep_ref[r * rows : (r + 1) * rows] = block
        else:
            at = (r - nodes // 2) * rows
            send_ref[at : at + rows] = block.astype(BF16)
    send_ref[nodes // 2 * rows :] = node
    keep_ref[nodes // 2 * rows :] = node.astype(F32)
    for copy in copies[5:]:
        copy.wait()


def top_kernel(src_hbm, top_ref, down_ref, matrix_ref, src_ref, by_node, sem):
    copy = pltpu.make_async_copy(src_hbm, src_ref, sem.at[0])
    copy.start()
    rank = down_ref.shape[1]
    me = lax.axis_index(NODE_AXES)
    by_node[...] = jnp.zeros_like(by_node)
    through = lax.dot_general(top_ref[0], down_ref[0], TN, preferred_element_type=F32)
    copy.wait()
    for k in range(src_ref.shape[1]):
        by_node[src_ref[0, k] ^ me] += through[k * rank : (k + 1) * rank]
    matrix_ref[...] = by_node[...].reshape(matrix_ref.shape).astype(BF16)


def near_kernel(src_hbm, adj_ref, a_ref, b_ref, tiles_ref, near_ref, src_ref, around, sem):
    copy = pltpu.make_async_copy(src_hbm, src_ref, sem.at[0])
    copy.start()
    leaf_dev, vectors, cells = adj_ref.shape
    me = lax.axis_index(NODE_AXES)
    around[:leaf_dev] = adj_ref[...]
    around[leaf_dev : 2 * leaf_dev] = a_ref[...]
    around[2 * leaf_dev :] = b_ref[...]
    copy.wait()
    for j in range(leaf_dev):
        total = None
        for k in range(src_ref.shape[1]):
            source = src_ref[j, k]
            node = source // leaf_dev
            base = jnp.where(node == me, 0, jnp.where(node == (me ^ 1), leaf_dev, 2 * leaf_dev))
            block = around[base + source % leaf_dev]
            part = jnp.dot(block, tiles_ref[j, k * cells : (k + 1) * cells], preferred_element_type=F32)
            total = part if total is None else total + part
        near_ref[j] = total


def final_kernel(got_ref, kept_ref, matrix_ref, in_ref, near_ref, out_ref):
    leaf_dev, vectors, _ = near_ref.shape
    rank = in_ref.shape[1]
    rows = leaf_dev // 2 * vectors
    coefs = [side_by_side(kept_ref[rows:].astype(BF16), vectors), side_by_side(got_ref[rows:], vectors)]
    down = jnp.dot(jnp.concatenate(coefs, axis=1), matrix_ref[...], preferred_element_type=F32)
    leaf_in = side_by_side(kept_ref[:rows] + got_ref[:rows].astype(F32), vectors)
    mixed = (leaf_in + down).astype(BF16)
    for j in range(leaf_dev):
        far = jnp.dot(mixed[:, j * rank : (j + 1) * rank], in_ref[j], preferred_element_type=F32)
        out_ref[j] = near_ref[j] + far


def on_device(
    adjoint, leaf_basis_out, leaf_basis_in, transfer_up, transfer_down, far_coupling, top_coupling, near_tiles, near_src, far_dst, top_src
):
    leaf_dev, vectors, cells = adjoint.shape
    rank = leaf_basis_out.shape[1]
    wide = 2 * rank
    pairs = leaf_dev // 2
    rows = pairs * vectors
    nodes = lax.axis_size(NODE_AXES)
    steps = bits_of(nodes)

    cores = lax.axis_size("sub")

    def swapped(x, partner, flip):
        pairs = [(i * cores + c, partner(i) * cores + (cores - 1 - c if flip else c)) for i in range(nodes) for c in range(cores)]
        return lax.ppermute(x, NODE_AXES + ("sub",), pairs)

    def like(x):
        return jax.ShapeDtypeStruct(x.shape, x.dtype)

    later = (near_tiles, top_coupling, transfer_down, leaf_basis_in)
    send, keep, adjoint_v, tiles, top, down, basis_in = pl.pallas_call(
        functools.partial(source_kernel, nodes),
        out_shape=(
            jax.ShapeDtypeStruct((nodes // 2 * rows + vectors, wide), BF16),
            jax.ShapeDtypeStruct((nodes // 2 * rows + vectors, wide), F32),
            like(adjoint),
            *map(like, later),
        ),
        in_specs=[HBM] * 9,
        out_specs=(VMEM,) * 7,
        scratch_shapes=[
            pltpu.SMEM(far_dst.shape, jnp.int32),
            pltpu.VMEM(leaf_basis_out.shape, BF16),
            pltpu.VMEM(far_coupling.shape, BF16),
            pltpu.VMEM(transfer_up.shape, BF16),
            pltpu.VMEM((leaf_dev, nodes * pairs, vectors, wide), F32),
            pltpu.SemaphoreType.DMA((9,)),
        ],
        compiler_params=PARAMS,
        name="source",
    )(*map(in_hbm, (far_dst, adjoint, leaf_basis_out, far_coupling, transfer_up, *later)))

    matrix = pl.pallas_call(
        top_kernel,
        out_shape=jax.ShapeDtypeStruct((nodes * rank, leaf_dev * rank), BF16),
        in_specs=[HBM] + [VMEM] * 2,
        out_specs=VMEM,
        scratch_shapes=[
            pltpu.SMEM(top_src.shape, jnp.int32),
            pltpu.VMEM((nodes, rank, leaf_dev * rank), F32),
            pltpu.SemaphoreType.DMA((1,)),
        ],
        compiler_params=PARAMS,
        name="top",
    )(in_hbm(top_src), top, down)

    inner = [(i, i + 1 if i % 2 else i - 1) for i in range(1, nodes - 1)]
    other = [(i * cores + c, j * cores + c) for i, j in inner for c in range(cores)]
    other += [(i * cores + c, i * cores + (c + 1) % cores) for i in (0, nodes - 1) for c in range(cores)]
    a = swapped(adjoint_v, lambda i: i ^ 1, False)
    b = lax.ppermute(lax.optimization_barrier((adjoint_v, a, matrix))[0], NODE_AXES + ("sub",), other)

    coefs = None
    for step in range(steps):
        flip = step in (0, steps - 1)
        half = (nodes >> (step + 1)) * rows
        if step:
            send = jnp.concatenate([keep[half:].astype(BF16)] + coefs, axis=0)
            keep = keep[:half]
            if flip:
                keep = jnp.concatenate([keep] + [coef.astype(F32) for coef in coefs], axis=0)
        got = swapped(send, lambda i: i ^ (1 << step), flip)
        if flip:
            keep = swapped(keep, lambda i: i, True)
        if step == 0:
            coefs = [jnp.where(jnp.arange(wide) < rank, keep[half:].astype(BF16), got[half:])]
        elif step < steps - 1:
            coefs.append(got[half:])
        if step < steps - 1:
            keep = keep[:half] + got[:half].astype(F32)

    near = pl.pallas_call(
        near_kernel,
        out_shape=jax.ShapeDtypeStruct((leaf_dev, vectors, cells), F32),
        in_specs=[HBM] + [VMEM] * 4,
        out_specs=VMEM,
        scratch_shapes=[
            pltpu.SMEM(near_src.shape, jnp.int32),
            pltpu.VMEM((3 * leaf_dev, vectors, cells), BF16),
            pltpu.SemaphoreType.DMA((1,)),
        ],
        compiler_params=PARAMS,
        name="near",
    )(in_hbm(near_src), adjoint_v, a, b, tiles)

    return pl.pallas_call(
        final_kernel,
        out_shape=jax.ShapeDtypeStruct((leaf_dev, vectors, cells), F32),
        in_specs=[VMEM] * 5,
        out_specs=VMEM,
        compiler_params=PARAMS,
        name="final",
    )(got, keep, matrix, basis_in, near)


def solution(mesh):
    split = P(("design", "leaf", "vec"), None, None)
    in_specs = (P(("design", "leaf", "vec"), "sub", None),) + (split,) * 7 + (P(("design", "leaf", "vec"), None),) * 3
    out_specs = P(("design", "leaf", "vec"), "sub", None)
    return jax.shard_map(on_device, mesh=mesh, in_specs=in_specs, out_specs=out_specs, check_vma=False)
```

```python
import functools

import jax
import jax.numpy as jnp
from jax import lax
from jax.experimental import pallas as pl
from jax.experimental.pallas import tpu as pltpu
from jax.sharding import PartitionSpec as P

F32 = jnp.float32
BF16 = jnp.bfloat16
NODE_AXES = ("leaf", "vec")
NT = (((1,), (1,)), ((), ()))
TN = (((0,), (0,)), ((), ()))
VMEM = pl.BlockSpec(memory_space=pltpu.VMEM)
HBM = pl.BlockSpec(memory_space=pltpu.HBM)
PARAMS = pltpu.CompilerParams(vmem_limit_bytes=32 << 20)


def bits_of(count):
    return count.bit_length() - 1


def reversed_bits(value, width):
    return sum(((value >> bit) & 1) << (width - 1 - bit) for bit in range(width))


def lane_half(shape):
    return lax.broadcasted_iota(jnp.int32, shape, 1) // (shape[1] // 2)


def in_hbm(x):
    return pltpu.with_memory_space_constraint(x, pltpu.HBM)


def side_by_side(stacked, rows):
    return jnp.concatenate([stacked[at : at + rows] for at in range(0, stacked.shape[0], rows)], axis=1)


def source_kernel(nodes, *refs):
    sources, (send_ref, keep_ref, adj_ref, *later), scratch = refs[:8], refs[8:14], refs[14:]
    dst_ref, out_ref, far_ref, up_ref, *sums, sems = scratch
    first = later[2].shape[0]
    sources = (*sources[:7], sources[7].at[:first])
    copies = [
        pltpu.make_async_copy(there, here, sems.at[i])
        for i, (there, here) in enumerate(zip(sources, (dst_ref, adj_ref, out_ref, far_ref, up_ref, *later)))
    ]
    for copy in copies:
        copy.start()
    leaf_dev, vectors, _ = adj_ref.shape
    rank = out_ref.shape[1]
    far_count = dst_ref.shape[1]
    pairs = leaf_dev // 2
    wide = 2 * rank
    within = bits_of(leaf_dev)
    me = lax.axis_index(NODE_AXES)
    rows = pairs * vectors
    for one in sums:
        one[...] = jnp.zeros_like(one)
    half = lane_half((vectors, wide))
    for copy in copies[:3]:
        copy.wait()
    coefs = [
        lax.dot_general(adj_ref[j], out_ref[j], NT, preferred_element_type=F32).astype(BF16) for j in range(leaf_dev)
    ]
    for copy in copies[3:5]:
        copy.wait()
    node = lax.dot_general(jnp.concatenate(coefs, axis=1), up_ref[0], NT, preferred_element_type=F32).astype(BF16)
    node = jnp.concatenate([node, node], axis=1)
    send_ref[nodes // 2 * rows :] = node
    keep_ref[nodes // 2 * rows :] = node.astype(F32)
    for j in range(leaf_dev):
        contrib = jnp.dot(coefs[j], far_ref[j], preferred_element_type=F32)
        for k in range(far_count):
            block = contrib[:, k // 2 * wide : (k // 2 + 1) * wide]
            target = dst_ref[j, k]
            place = ((target >> within) ^ me) * pairs + ((target & (leaf_dev - 1)) >> 1)
            place += ((target ^ k) & 1) * (nodes * pairs)
            sums[j][place] += jnp.where(half == k % 2, block, 0.0)
    width = bits_of(nodes)
    for r in range(nodes):
        for p in range(pairs):
            place = reversed_bits(r, width) * pairs + p
            straight = sum(one[place] for one in sums)
            turned = sum(one[nodes * pairs + place] for one in sums)
            block = straight + pltpu.roll(turned, rank, 1)
            at = (r % (nodes // 2)) * rows + p * vectors
            if r < nodes // 2:
                keep_ref[at : at + vectors] = block
            else:
                send_ref[at : at + vectors] = block.astype(BF16)
    for copy in copies[5:]:
        copy.wait()


def top_kernel(src_hbm, top_ref, down_ref, tiles_hbm, in_hbm_ref, matrix_ref, tiles_ref, in_ref, src_ref, by_node, sems):
    sources = (src_hbm, tiles_hbm.at[tiles_hbm.shape[0] - tiles_ref.shape[0] :], in_hbm_ref)
    copies = [
        pltpu.make_async_copy(there, here, sems.at[i]) for i, (there, here) in enumerate(zip(sources, (src_ref, tiles_ref, in_ref)))
    ]
    for copy in copies:
        copy.start()
    rank = down_ref.shape[1]
    me = lax.axis_index(NODE_AXES)
    by_node[...] = jnp.zeros_like(by_node)
    through = lax.dot_general(top_ref[0], down_ref[0], TN, preferred_element_type=F32)
    copies[0].wait()
    for k in range(src_ref.shape[1]):
        by_node[src_ref[0, k] ^ me] += through[k * rank : (k + 1) * rank]
    matrix_ref[...] = by_node[...].reshape(matrix_ref.shape).astype(BF16)
    for copy in copies[1:]:
        copy.wait()


def near_kernel(src_hbm, adj_ref, a_ref, b_ref, tiles_ref, more_tiles_ref, near_ref, src_ref, around, sem):
    copy = pltpu.make_async_copy(src_hbm, src_ref, sem.at[0])
    copy.start()
    leaf_dev, vectors, cells = adj_ref.shape
    me = lax.axis_index(NODE_AXES)
    first = tiles_ref.shape[0]
    around[:leaf_dev] = adj_ref[...]
    around[leaf_dev : 2 * leaf_dev] = a_ref[...]
    around[2 * leaf_dev :] = b_ref[...]
    copy.wait()
    for j in range(leaf_dev):
        total = None
        for k in range(src_ref.shape[1]):
            source = src_ref[j, k]
            node = source // leaf_dev
            base = jnp.where(node == me, 0, jnp.where(node == (me ^ 1), leaf_dev, 2 * leaf_dev))
            block = around[base + source % leaf_dev]
            tiles, at = (tiles_ref, j) if j < first else (more_tiles_ref, j - first)
            part = jnp.dot(block, tiles[at, k * cells : (k + 1) * cells], preferred_element_type=F32)
            total = part if total is None else total + part
        near_ref[j] = total


def final_kernel(got_ref, kept_ref, matrix_ref, in_ref, near_ref, out_ref):
    leaf_dev, vectors, _ = near_ref.shape
    rank = in_ref.shape[1]
    rows = leaf_dev // 2 * vectors
    coefs = [side_by_side(kept_ref[rows:].astype(BF16), vectors), side_by_side(got_ref[rows:], vectors)]
    down = jnp.dot(jnp.concatenate(coefs, axis=1), matrix_ref[...], preferred_element_type=F32)
    leaf_in = side_by_side(kept_ref[:rows] + got_ref[:rows].astype(F32), vectors)
    mixed = (leaf_in + down).astype(BF16)
    for j in range(leaf_dev):
        far = jnp.dot(mixed[:, j * rank : (j + 1) * rank], in_ref[j], preferred_element_type=F32)
        out_ref[j] = near_ref[j] + far


def on_device(
    adjoint, leaf_basis_out, leaf_basis_in, transfer_up, transfer_down, far_coupling, top_coupling, near_tiles, near_src, far_dst, top_src
):
    leaf_dev, vectors, cells = adjoint.shape
    rank = leaf_basis_out.shape[1]
    wide = 2 * rank
    pairs = leaf_dev // 2
    rows = pairs * vectors
    nodes = lax.axis_size(NODE_AXES)
    steps = bits_of(nodes)

    cores = lax.axis_size("sub")

    def swapped(x, partner, flip):
        pairs = [(i * cores + c, partner(i) * cores + (cores - 1 - c if flip else c)) for i in range(nodes) for c in range(cores)]
        return lax.ppermute(x, NODE_AXES + ("sub",), pairs)

    def like(x):
        return jax.ShapeDtypeStruct(x.shape, x.dtype)

    first = leaf_dev // 2
    tiles_shape = (first,) + near_tiles.shape[1:]
    more_shape = (leaf_dev - first,) + near_tiles.shape[1:]
    send, keep, adjoint_v, top, down, tiles = pl.pallas_call(
        functools.partial(source_kernel, nodes),
        out_shape=(
            jax.ShapeDtypeStruct((nodes // 2 * rows + vectors, wide), BF16),
            jax.ShapeDtypeStruct((nodes // 2 * rows + vectors, wide), F32),
            like(adjoint),
            like(top_coupling),
            like(transfer_down),
            jax.ShapeDtypeStruct(tiles_shape, BF16),
        ),
        in_specs=[HBM] * 8,
        out_specs=(VMEM,) * 6,
        scratch_shapes=[
            pltpu.SMEM(far_dst.shape, jnp.int32),
            pltpu.VMEM(leaf_basis_out.shape, BF16),
            pltpu.VMEM(far_coupling.shape, BF16),
            pltpu.VMEM(transfer_up.shape, BF16),
            *[pltpu.VMEM((2 * nodes * pairs, vectors, wide), F32)] * leaf_dev,
            pltpu.SemaphoreType.DMA((8,)),
        ],
        compiler_params=PARAMS,
        name="source",
    )(*map(in_hbm, (far_dst, adjoint, leaf_basis_out, far_coupling, transfer_up, top_coupling, transfer_down, near_tiles)))

    matrix, more_tiles, basis_in = pl.pallas_call(
        top_kernel,
        out_shape=(
            jax.ShapeDtypeStruct((nodes * rank, leaf_dev * rank), BF16),
            jax.ShapeDtypeStruct(more_shape, BF16),
            like(leaf_basis_in),
        ),
        in_specs=[HBM] + [VMEM] * 2 + [HBM] * 2,
        out_specs=(VMEM,) * 3,
        scratch_shapes=[
            pltpu.SMEM(top_src.shape, jnp.int32),
            pltpu.VMEM((nodes, rank, leaf_dev * rank), F32),
            pltpu.SemaphoreType.DMA((3,)),
        ],
        compiler_params=PARAMS,
        name="top",
    )(in_hbm(top_src), top, down, in_hbm(near_tiles), in_hbm(leaf_basis_in))

    inner = [(i, i + 1 if i % 2 else i - 1) for i in range(1, nodes - 1)]
    other = [(i * cores + c, j * cores + c) for i, j in inner for c in range(cores)]
    other += [(i * cores + c, i * cores + (c + 1) % cores) for i in (0, nodes - 1) for c in range(cores)]
    send, _ = lax.optimization_barrier((send, keep))
    a = swapped(lax.optimization_barrier((adjoint_v, send, keep))[0], lambda i: i ^ 1, False)
    b = lax.ppermute(lax.optimization_barrier((adjoint_v, a))[0], NODE_AXES + ("sub",), other)

    coefs = None
    for step in range(steps):
        flip = step in (0, steps - 1)
        half = (nodes >> (step + 1)) * rows
        if step:
            send = jnp.concatenate([keep[half:].astype(BF16)] + coefs, axis=0)
            keep = keep[:half]
            if flip:
                keep = jnp.concatenate([keep] + [coef.astype(F32) for coef in coefs], axis=0)
        got = swapped(send, lambda i: i ^ (1 << step), flip)
        if flip:
            keep = swapped(keep, lambda i: i, True)
        if step == 0:
            got, _ = lax.optimization_barrier((got, matrix))
            coefs = [jnp.where(jnp.arange(wide) < rank, keep[half:].astype(BF16), got[half:])]
        elif step < steps - 1:
            coefs.append(got[half:])
        if step < steps - 1:
            keep = keep[:half] + got[:half].astype(F32)

    near = pl.pallas_call(
        near_kernel,
        out_shape=jax.ShapeDtypeStruct((leaf_dev, vectors, cells), F32),
        in_specs=[HBM] + [VMEM] * 5,
        out_specs=VMEM,
        scratch_shapes=[
            pltpu.SMEM(near_src.shape, jnp.int32),
            pltpu.VMEM((3 * leaf_dev, vectors, cells), BF16),
            pltpu.SemaphoreType.DMA((1,)),
        ],
        compiler_params=PARAMS,
        name="near",
    )(in_hbm(near_src), adjoint_v, a, b, tiles, more_tiles)

    return pl.pallas_call(
        final_kernel,
        out_shape=jax.ShapeDtypeStruct((leaf_dev, vectors, cells), F32),
        in_specs=[VMEM] * 5,
        out_specs=VMEM,
        compiler_params=PARAMS,
        name="final",
    )(got, keep, matrix, basis_in, near)


def solution(mesh):
    split = P(("design", "leaf", "vec"), None, None)
    in_specs = (P(("design", "leaf", "vec"), "sub", None),) + (split,) * 7 + (P(("design", "leaf", "vec"), None),) * 3
    out_specs = P(("design", "leaf", "vec"), "sub", None)
    return jax.shard_map(on_device, mesh=mesh, in_specs=in_specs, out_specs=out_specs, check_vma=False)
```

```python
import functools

import jax
import jax.numpy as jnp
from jax import lax
from jax.experimental import pallas as pl
from jax.experimental.pallas import tpu as pltpu
from jax.sharding import PartitionSpec as P

F32 = jnp.float32
BF16 = jnp.bfloat16
NODE_AXES = ("leaf", "vec")
NT = (((1,), (1,)), ((), ()))
TN = (((0,), (0,)), ((), ()))
VMEM = pl.BlockSpec(memory_space=pltpu.VMEM)
HBM = pl.BlockSpec(memory_space=pltpu.HBM)
PARAMS = pltpu.CompilerParams(vmem_limit_bytes=32 << 20)


def bits_of(count):
    return count.bit_length() - 1


def reversed_bits(value, width):
    return sum(((value >> bit) & 1) << (width - 1 - bit) for bit in range(width))


def lane_half(shape):
    return lax.broadcasted_iota(jnp.int32, shape, 1) // (shape[1] // 2)


def in_hbm(x):
    return pltpu.with_memory_space_constraint(x, pltpu.HBM)


def side_by_side(stacked, rows):
    return jnp.concatenate([stacked[at : at + rows] for at in range(0, stacked.shape[0], rows)], axis=1)


def source_kernel(nodes, *refs):
    sources, (send_ref, keep_ref, adj_ref, *later), scratch = refs[:8], refs[8:14], refs[14:]
    dst_ref, out_ref, far_ref, up_ref, *sums, sems = scratch
    first = later[2].shape[0]
    sources = (*sources[:7], sources[7].at[:first])
    copies = [
        pltpu.make_async_copy(there, here, sems.at[i])
        for i, (there, here) in enumerate(zip(sources, (dst_ref, adj_ref, out_ref, far_ref, up_ref, *later)))
    ]
    for copy in copies:
        copy.start()
    leaf_dev, vectors, _ = adj_ref.shape
    rank = out_ref.shape[1]
    far_count = dst_ref.shape[1]
    pairs = leaf_dev // 2
    wide = 2 * rank
    within = bits_of(leaf_dev)
    me = lax.axis_index(NODE_AXES)
    rows = pairs * vectors
    for one in sums:
        one[...] = jnp.zeros_like(one)
    half = lane_half((vectors, wide))
    for copy in copies[:3]:
        copy.wait()
    coefs = [
        lax.dot_general(adj_ref[j], out_ref[j], NT, preferred_element_type=F32).astype(BF16) for j in range(leaf_dev)
    ]
    for copy in copies[3:5]:
        copy.wait()
    node = lax.dot_general(jnp.concatenate(coefs, axis=1), up_ref[0], NT, preferred_element_type=F32).astype(BF16)
    node = jnp.concatenate([node, node], axis=1)
    send_ref[nodes // 2 * rows :] = node
    keep_ref[nodes // 2 * rows :] = node.astype(F32)
    for j in range(leaf_dev):
        contrib = jnp.dot(coefs[j], far_ref[j], preferred_element_type=F32)
        for k in range(far_count):
            block = contrib[:, k // 2 * wide : (k // 2 + 1) * wide]
            target = dst_ref[j, k]
            place = ((target >> within) ^ me) * pairs + ((target & (leaf_dev - 1)) >> 1)
            place += ((target ^ k) & 1) * (nodes * pairs)
            sums[j][place] += jnp.where(half == k % 2, block, 0.0)
    width = bits_of(nodes)
    for r in range(nodes):
        for p in range(pairs):
            place = reversed_bits(r, width) * pairs + p
            straight = sum(one[place] for one in sums)
            turned = sum(one[nodes * pairs + place] for one in sums)
            block = straight + pltpu.roll(turned, rank, 1)
            at = (r % (nodes // 2)) * rows + p * vectors
            if r < nodes // 2:
                keep_ref[at : at + vectors] = block
            else:
                send_ref[at : at + vectors] = block.astype(BF16)
    for copy in copies[5:]:
        copy.wait()


def top_kernel(src_hbm, top_ref, down_ref, tiles_hbm, in_hbm_ref, matrix_ref, tiles_ref, in_ref, src_ref, by_node, sems):
    sources = (src_hbm, tiles_hbm.at[tiles_hbm.shape[0] - tiles_ref.shape[0] :], in_hbm_ref)
    copies = [
        pltpu.make_async_copy(there, here, sems.at[i]) for i, (there, here) in enumerate(zip(sources, (src_ref, tiles_ref, in_ref)))
    ]
    for copy in copies:
        copy.start()
    rank = down_ref.shape[1]
    me = lax.axis_index(NODE_AXES)
    by_node[...] = jnp.zeros_like(by_node)
    through = lax.dot_general(top_ref[0], down_ref[0], TN, preferred_element_type=F32)
    copies[0].wait()
    for k in range(src_ref.shape[1]):
        by_node[src_ref[0, k] ^ me] += through[k * rank : (k + 1) * rank]
    matrix_ref[...] = by_node[...].reshape(matrix_ref.shape).astype(BF16)
    for copy in copies[1:]:
        copy.wait()


def fold_kernel(matrix_ref, in_ref, folded_ref):
    leaf_dev, rank, cells = in_ref.shape
    known = matrix_ref.shape[0] - folded_ref.shape[0]
    for j in range(leaf_dev):
        block = matrix_ref[known:, j * rank : (j + 1) * rank]
        folded_ref[:, j * cells : (j + 1) * cells] = jnp.dot(block, in_ref[j], preferred_element_type=F32).astype(BF16)


def near_kernel(src_hbm, adj_ref, a_ref, b_ref, tiles_ref, more_tiles_ref, kept_ref, matrix_ref, in_ref, base_ref, src_ref, around, sem):
    copy = pltpu.make_async_copy(src_hbm, src_ref, sem.at[0])
    copy.start()
    leaf_dev, vectors, cells = adj_ref.shape
    rank = in_ref.shape[1]
    rows = leaf_dev // 2 * vectors
    first = tiles_ref.shape[0]
    me = lax.axis_index(NODE_AXES)
    around[:leaf_dev] = adj_ref[...]
    around[leaf_dev : 2 * leaf_dev] = a_ref[...]
    around[2 * leaf_dev :] = b_ref[...]
    coefs = side_by_side(kept_ref[rows:].astype(BF16), vectors)
    down = jnp.dot(coefs, matrix_ref[: coefs.shape[1]], preferred_element_type=F32)
    mixed = (side_by_side(kept_ref[:rows], vectors) + down).astype(BF16)
    copy.wait()
    for j in range(leaf_dev):
        total = jnp.dot(mixed[:, j * rank : (j + 1) * rank], in_ref[j], preferred_element_type=F32)
        for k in range(src_ref.shape[1]):
            source = src_ref[j, k]
            node = source // leaf_dev
            base = jnp.where(node == me, 0, jnp.where(node == (me ^ 1), leaf_dev, 2 * leaf_dev))
            block = around[base + source % leaf_dev]
            tiles, at = (tiles_ref, j) if j < first else (more_tiles_ref, j - first)
            total += jnp.dot(block, tiles[at, k * cells : (k + 1) * cells], preferred_element_type=F32)
        base_ref[j] = total


def final_kernel(got_ref, folded_ref, in_ref, base_ref, out_ref):
    leaf_dev, vectors, cells = base_ref.shape
    rank = in_ref.shape[1]
    rows = leaf_dev // 2 * vectors
    coefs = side_by_side(got_ref[rows:], vectors)
    mixed = side_by_side(got_ref[:rows], vectors)
    for j in range(leaf_dev):
        top = jnp.dot(coefs, folded_ref[:, j * cells : (j + 1) * cells], preferred_element_type=F32)
        far = jnp.dot(mixed[:, j * rank : (j + 1) * rank], in_ref[j], preferred_element_type=F32)
        out_ref[j] = base_ref[j] + (top + far)


def on_device(
    adjoint, leaf_basis_out, leaf_basis_in, transfer_up, transfer_down, far_coupling, top_coupling, near_tiles, near_src, far_dst, top_src
):
    leaf_dev, vectors, cells = adjoint.shape
    rank = leaf_basis_out.shape[1]
    wide = 2 * rank
    pairs = leaf_dev // 2
    rows = pairs * vectors
    nodes = lax.axis_size(NODE_AXES)
    steps = bits_of(nodes)

    cores = lax.axis_size("sub")

    def swapped(x, partner, flip):
        pairs = [(i * cores + c, partner(i) * cores + (cores - 1 - c if flip else c)) for i in range(nodes) for c in range(cores)]
        return lax.ppermute(x, NODE_AXES + ("sub",), pairs)

    def like(x):
        return jax.ShapeDtypeStruct(x.shape, x.dtype)

    first = leaf_dev // 2
    tiles_shape = (first,) + near_tiles.shape[1:]
    more_shape = (leaf_dev - first,) + near_tiles.shape[1:]
    send, keep, adjoint_v, top, down, tiles = pl.pallas_call(
        functools.partial(source_kernel, nodes),
        out_shape=(
            jax.ShapeDtypeStruct((nodes // 2 * rows + vectors, wide), BF16),
            jax.ShapeDtypeStruct((nodes // 2 * rows + vectors, wide), F32),
            like(adjoint),
            like(top_coupling),
            like(transfer_down),
            jax.ShapeDtypeStruct(tiles_shape, BF16),
        ),
        in_specs=[HBM] * 8,
        out_specs=(VMEM,) * 6,
        scratch_shapes=[
            pltpu.SMEM(far_dst.shape, jnp.int32),
            pltpu.VMEM(leaf_basis_out.shape, BF16),
            pltpu.VMEM(far_coupling.shape, BF16),
            pltpu.VMEM(transfer_up.shape, BF16),
            *[pltpu.VMEM((2 * nodes * pairs, vectors, wide), F32)] * leaf_dev,
            pltpu.SemaphoreType.DMA((8,)),
        ],
        compiler_params=PARAMS,
        name="source",
    )(*map(in_hbm, (far_dst, adjoint, leaf_basis_out, far_coupling, transfer_up, top_coupling, transfer_down, near_tiles)))

    matrix, more_tiles, basis_in = pl.pallas_call(
        top_kernel,
        out_shape=(
            jax.ShapeDtypeStruct((nodes * rank, leaf_dev * rank), BF16),
            jax.ShapeDtypeStruct(more_shape, BF16),
            like(leaf_basis_in),
        ),
        in_specs=[HBM] + [VMEM] * 2 + [HBM] * 2,
        out_specs=(VMEM,) * 3,
        scratch_shapes=[
            pltpu.SMEM(top_src.shape, jnp.int32),
            pltpu.VMEM((nodes, rank, leaf_dev * rank), F32),
            pltpu.SemaphoreType.DMA((3,)),
        ],
        compiler_params=PARAMS,
        name="top",
    )(in_hbm(top_src), top, down, in_hbm(near_tiles), in_hbm(leaf_basis_in))

    folded = pl.pallas_call(
        fold_kernel,
        out_shape=jax.ShapeDtypeStruct((nodes // 2 * rank, leaf_dev * cells), BF16),
        in_specs=[VMEM] * 2,
        out_specs=VMEM,
        compiler_params=PARAMS,
        name="fold",
    )(matrix, basis_in)

    inner = [(i, i + 1 if i % 2 else i - 1) for i in range(1, nodes - 1)]
    other = [(i * cores + c, j * cores + c) for i, j in inner for c in range(cores)]
    other += [(i * cores + c, i * cores + (c + 1) % cores) for i in (0, nodes - 1) for c in range(cores)]
    send, _ = lax.optimization_barrier((send, keep))
    a = swapped(lax.optimization_barrier((adjoint_v, send, keep))[0], lambda i: i ^ 1, False)
    b = lax.ppermute(lax.optimization_barrier((adjoint_v, a, folded))[0], NODE_AXES + ("sub",), other)

    coefs = None
    for step in range(steps):
        flip = step in (0, steps - 1)
        half = (nodes >> (step + 1)) * rows
        if step:
            send = jnp.concatenate([keep[half:].astype(BF16)] + coefs, axis=0)
            keep = keep[:half]
            if flip:
                keep = jnp.concatenate([keep] + [coef.astype(F32) for coef in coefs], axis=0)
        got = swapped(send, lambda i: i ^ (1 << step), flip)
        if flip:
            keep = swapped(keep, lambda i: i, True)
        if step == 0:
            got, _ = lax.optimization_barrier((got, matrix))
            coefs = [jnp.where(jnp.arange(wide) < rank, keep[half:].astype(BF16), got[half:])]
        elif step < steps - 1:
            coefs.append(got[half:])
        if step < steps - 1:
            keep = keep[:half] + got[:half].astype(F32)

    base = pl.pallas_call(
        near_kernel,
        out_shape=jax.ShapeDtypeStruct((leaf_dev, vectors, cells), F32),
        in_specs=[HBM] + [VMEM] * 8,
        out_specs=VMEM,
        scratch_shapes=[
            pltpu.SMEM(near_src.shape, jnp.int32),
            pltpu.VMEM((3 * leaf_dev, vectors, cells), BF16),
            pltpu.SemaphoreType.DMA((1,)),
        ],
        compiler_params=PARAMS,
        name="near",
    )(in_hbm(near_src), adjoint_v, a, b, tiles, more_tiles, keep, matrix, basis_in)

    return pl.pallas_call(
        final_kernel,
        out_shape=jax.ShapeDtypeStruct((leaf_dev, vectors, cells), F32),
        in_specs=[VMEM] * 4,
        out_specs=VMEM,
        compiler_params=PARAMS,
        name="final",
    )(got, folded, basis_in, base)


def solution(mesh):
    split = P(("design", "leaf", "vec"), None, None)
    in_specs = (P(("design", "leaf", "vec"), "sub", None),) + (split,) * 7 + (P(("design", "leaf", "vec"), None),) * 3
    out_specs = P(("design", "leaf", "vec"), "sub", None)
    return jax.shard_map(on_device, mesh=mesh, in_specs=in_specs, out_specs=out_specs, check_vma=False)
```

```python
import functools

import jax
import jax.numpy as jnp
from jax import lax
from jax.experimental import pallas as pl
from jax.experimental.pallas import tpu as pltpu
from jax.sharding import PartitionSpec as P

F32 = jnp.float32
BF16 = jnp.bfloat16
NODE_AXES = ("leaf", "vec")
NT = (((1,), (1,)), ((), ()))
TN = (((0,), (0,)), ((), ()))
VMEM = pl.BlockSpec(memory_space=pltpu.VMEM)
HBM = pl.BlockSpec(memory_space=pltpu.HBM)
PARAMS = pltpu.CompilerParams(vmem_limit_bytes=32 << 20)


def bits_of(count):
    return count.bit_length() - 1


def reversed_bits(value, width):
    return sum(((value >> bit) & 1) << (width - 1 - bit) for bit in range(width))


def lane_half(shape):
    return lax.broadcasted_iota(jnp.int32, shape, 1) // (shape[1] // 2)


def in_hbm(x):
    return pltpu.with_memory_space_constraint(x, pltpu.HBM)


def side_by_side(stacked, rows):
    return jnp.concatenate([stacked[at : at + rows] for at in range(0, stacked.shape[0], rows)], axis=1)


def source_kernel(nodes, *refs):
    sources, (send_ref, keep_ref, adj_ref, *later), scratch = refs[:8], refs[8:14], refs[14:]
    dst_ref, out_ref, far_ref, up_ref, *sums, sems = scratch
    first = later[2].shape[0]
    sources = (*sources[:7], sources[7].at[:first])
    copies = [
        pltpu.make_async_copy(there, here, sems.at[i])
        for i, (there, here) in enumerate(zip(sources, (dst_ref, adj_ref, out_ref, far_ref, up_ref, *later)))
    ]
    for copy in copies:
        copy.start()
    leaf_dev, vectors, _ = adj_ref.shape
    rank = out_ref.shape[1]
    far_count = dst_ref.shape[1]
    pairs = leaf_dev // 2
    wide = 2 * rank
    within = bits_of(leaf_dev)
    me = lax.axis_index(NODE_AXES)
    rows = pairs * vectors
    for one in sums:
        one[...] = jnp.zeros_like(one)
    half = lane_half((vectors, wide))
    for copy in copies[:3]:
        copy.wait()
    coefs = [
        lax.dot_general(adj_ref[j], out_ref[j], NT, preferred_element_type=F32).astype(BF16) for j in range(leaf_dev)
    ]
    for copy in copies[3:5]:
        copy.wait()
    for j in range(leaf_dev):
        contrib = jnp.dot(coefs[j], far_ref[j], preferred_element_type=F32)
        for k in range(far_count):
            block = contrib[:, k // 2 * wide : (k // 2 + 1) * wide]
            target = dst_ref[j, k]
            place = ((target >> within) ^ me) * pairs + ((target & (leaf_dev - 1)) >> 1)
            place += ((target ^ k) & 1) * (nodes * pairs)
            sums[j][place] += jnp.where(half == k % 2, block, 0.0)
    node = lax.dot_general(jnp.concatenate(coefs, axis=1), up_ref[0], NT, preferred_element_type=F32).astype(BF16)
    node = jnp.concatenate([node, node], axis=1)
    send_ref[nodes // 2 * rows :] = node
    keep_ref[nodes // 2 * rows :] = node.astype(F32)
    width = bits_of(nodes)
    for r in range(nodes):
        for p in range(pairs):
            place = reversed_bits(r, width) * pairs + p
            straight = sum(one[place] for one in sums)
            turned = sum(one[nodes * pairs + place] for one in sums)
            block = straight + pltpu.roll(turned, rank, 1)
            at = (r % (nodes // 2)) * rows + p * vectors
            if r < nodes // 2:
                keep_ref[at : at + vectors] = block
            else:
                send_ref[at : at + vectors] = block.astype(BF16)
    for copy in copies[5:]:
        copy.wait()


def top_kernel(src_hbm, top_ref, down_ref, tiles_hbm, in_hbm_ref, matrix_ref, rest_ref, tiles_ref, in_ref, src_ref, by_node, sems):
    sources = (src_hbm, tiles_hbm.at[tiles_hbm.shape[0] - tiles_ref.shape[0] :], in_hbm_ref)
    copies = [
        pltpu.make_async_copy(there, here, sems.at[i]) for i, (there, here) in enumerate(zip(sources, (src_ref, tiles_ref, in_ref)))
    ]
    for copy in copies:
        copy.start()
    rank = down_ref.shape[1]
    me = lax.axis_index(NODE_AXES)
    by_node[...] = jnp.zeros_like(by_node)
    through = lax.dot_general(top_ref[0], down_ref[0], TN, preferred_element_type=F32)
    copies[0].wait()
    for k in range(src_ref.shape[1]):
        by_node[src_ref[0, k] ^ me] += through[k * rank : (k + 1) * rank]
    matrix = by_node[...].reshape(matrix_ref.shape)
    rounded = matrix.astype(BF16)
    matrix_ref[...] = rounded
    rest_ref[...] = (matrix - rounded.astype(F32)).astype(BF16)
    for copy in copies[1:]:
        copy.wait()


def fold_kernel(matrix_ref, rest_ref, in_ref, folded_ref):
    leaf_dev, rank, cells = in_ref.shape
    known = matrix_ref.shape[0] - folded_ref.shape[0]
    for j in range(leaf_dev):
        blocks = [ref[known:, j * rank : (j + 1) * rank] for ref in (matrix_ref, rest_ref)]
        total = sum(jnp.dot(block, in_ref[j], preferred_element_type=F32) for block in blocks)
        folded_ref[:, j * cells : (j + 1) * cells] = total.astype(BF16)


def near_kernel(src_hbm, adj_ref, a_ref, b_ref, tiles_ref, more_tiles_ref, kept_ref, matrix_ref, rest_ref, in_ref, base_ref, src_ref, around, sem):
    copy = pltpu.make_async_copy(src_hbm, src_ref, sem.at[0])
    copy.start()
    leaf_dev, vectors, cells = adj_ref.shape
    rank = in_ref.shape[1]
    rows = leaf_dev // 2 * vectors
    first = tiles_ref.shape[0]
    me = lax.axis_index(NODE_AXES)
    around[:leaf_dev] = adj_ref[...]
    around[leaf_dev : 2 * leaf_dev] = a_ref[...]
    around[2 * leaf_dev :] = b_ref[...]
    coefs = side_by_side(kept_ref[rows:].astype(BF16), vectors)
    down = sum(jnp.dot(coefs, ref[: coefs.shape[1]], preferred_element_type=F32) for ref in (matrix_ref, rest_ref))
    mixed = (side_by_side(kept_ref[:rows], vectors) + down).astype(BF16)
    copy.wait()
    for j in range(leaf_dev):
        total = jnp.dot(mixed[:, j * rank : (j + 1) * rank], in_ref[j], preferred_element_type=F32)
        for k in range(src_ref.shape[1]):
            source = src_ref[j, k]
            node = source // leaf_dev
            base = jnp.where(node == me, 0, jnp.where(node == (me ^ 1), leaf_dev, 2 * leaf_dev))
            block = around[base + source % leaf_dev]
            tiles, at = (tiles_ref, j) if j < first else (more_tiles_ref, j - first)
            total += jnp.dot(block, tiles[at, k * cells : (k + 1) * cells], preferred_element_type=F32)
        base_ref[j] = total


def final_kernel(got_ref, folded_ref, in_ref, base_ref, out_ref):
    leaf_dev, vectors, cells = base_ref.shape
    rank = in_ref.shape[1]
    rows = leaf_dev // 2 * vectors
    coefs = side_by_side(got_ref[rows:], vectors)
    mixed = side_by_side(got_ref[:rows], vectors)
    for j in range(leaf_dev):
        top = jnp.dot(coefs, folded_ref[:, j * cells : (j + 1) * cells], preferred_element_type=F32)
        far = jnp.dot(mixed[:, j * rank : (j + 1) * rank], in_ref[j], preferred_element_type=F32)
        out_ref[j] = base_ref[j] + (top + far)


def on_device(
    adjoint, leaf_basis_out, leaf_basis_in, transfer_up, transfer_down, far_coupling, top_coupling, near_tiles, near_src, far_dst, top_src
):
    leaf_dev, vectors, cells = adjoint.shape
    rank = leaf_basis_out.shape[1]
    wide = 2 * rank
    pairs = leaf_dev // 2
    rows = pairs * vectors
    nodes = lax.axis_size(NODE_AXES)
    steps = bits_of(nodes)

    cores = lax.axis_size("sub")

    def swapped(x, partner, flip):
        pairs = [(i * cores + c, partner(i) * cores + (cores - 1 - c if flip else c)) for i in range(nodes) for c in range(cores)]
        return lax.ppermute(x, NODE_AXES + ("sub",), pairs)

    def like(x):
        return jax.ShapeDtypeStruct(x.shape, x.dtype)

    first = leaf_dev // 2
    tiles_shape = (first,) + near_tiles.shape[1:]
    more_shape = (leaf_dev - first,) + near_tiles.shape[1:]
    send, keep, adjoint_v, top, down, tiles = pl.pallas_call(
        functools.partial(source_kernel, nodes),
        out_shape=(
            jax.ShapeDtypeStruct((nodes // 2 * rows + vectors, wide), BF16),
            jax.ShapeDtypeStruct((nodes // 2 * rows + vectors, wide), F32),
            like(adjoint),
            like(top_coupling),
            like(transfer_down),
            jax.ShapeDtypeStruct(tiles_shape, BF16),
        ),
        in_specs=[HBM] * 8,
        out_specs=(VMEM,) * 6,
        scratch_shapes=[
            pltpu.SMEM(far_dst.shape, jnp.int32),
            pltpu.VMEM(leaf_basis_out.shape, BF16),
            pltpu.VMEM(far_coupling.shape, BF16),
            pltpu.VMEM(transfer_up.shape, BF16),
            *[pltpu.VMEM((2 * nodes * pairs, vectors, wide), F32)] * leaf_dev,
            pltpu.SemaphoreType.DMA((8,)),
        ],
        compiler_params=PARAMS,
        name="source",
    )(*map(in_hbm, (far_dst, adjoint, leaf_basis_out, far_coupling, transfer_up, top_coupling, transfer_down, near_tiles)))

    matrix, rest, more_tiles, basis_in = pl.pallas_call(
        top_kernel,
        out_shape=(
            jax.ShapeDtypeStruct((nodes * rank, leaf_dev * rank), BF16),
            jax.ShapeDtypeStruct((nodes * rank, leaf_dev * rank), BF16),
            jax.ShapeDtypeStruct(more_shape, BF16),
            like(leaf_basis_in),
        ),
        in_specs=[HBM] + [VMEM] * 2 + [HBM] * 2,
        out_specs=(VMEM,) * 4,
        scratch_shapes=[
            pltpu.SMEM(top_src.shape, jnp.int32),
            pltpu.VMEM((nodes, rank, leaf_dev * rank), F32),
            pltpu.SemaphoreType.DMA((3,)),
        ],
        compiler_params=PARAMS,
        name="top",
    )(in_hbm(top_src), top, down, in_hbm(near_tiles), in_hbm(leaf_basis_in))

    folded = pl.pallas_call(
        fold_kernel,
        out_shape=jax.ShapeDtypeStruct((nodes // 2 * rank, leaf_dev * cells), BF16),
        in_specs=[VMEM] * 3,
        out_specs=VMEM,
        compiler_params=PARAMS,
        name="fold",
    )(matrix, rest, basis_in)

    inner = [(i, i + 1 if i % 2 else i - 1) for i in range(1, nodes - 1)]
    other = [(i * cores + c, j * cores + c) for i, j in inner for c in range(cores)]
    other += [(i * cores + c, i * cores + (c + 1) % cores) for i in (0, nodes - 1) for c in range(cores)]
    send, _ = lax.optimization_barrier((send, keep))
    a = swapped(lax.optimization_barrier((adjoint_v, send, keep))[0], lambda i: i ^ 1, False)
    b = lax.ppermute(lax.optimization_barrier((adjoint_v, a, folded))[0], NODE_AXES + ("sub",), other)

    coefs = None
    for step in range(steps):
        flip = step in (0, steps - 1)
        half = (nodes >> (step + 1)) * rows
        if step:
            send = jnp.concatenate([keep[half:].astype(BF16)] + coefs, axis=0)
            keep = keep[:half]
            if flip:
                keep = jnp.concatenate([keep] + [coef.astype(F32) for coef in coefs], axis=0)
        got = swapped(send, lambda i: i ^ (1 << step), flip)
        if flip:
            keep = swapped(keep, lambda i: i, True)
        if step == 0:
            got, _ = lax.optimization_barrier((got, matrix))
            coefs = [jnp.where(jnp.arange(wide) < rank, keep[half:].astype(BF16), got[half:])]
        elif step < steps - 1:
            coefs.append(got[half:])
        if step < steps - 1:
            keep = keep[:half] + got[:half].astype(F32)

    base = pl.pallas_call(
        near_kernel,
        out_shape=jax.ShapeDtypeStruct((leaf_dev, vectors, cells), F32),
        in_specs=[HBM] + [VMEM] * 9,
        out_specs=VMEM,
        scratch_shapes=[
            pltpu.SMEM(near_src.shape, jnp.int32),
            pltpu.VMEM((3 * leaf_dev, vectors, cells), BF16),
            pltpu.SemaphoreType.DMA((1,)),
        ],
        compiler_params=PARAMS,
        name="near",
    )(in_hbm(near_src), adjoint_v, a, b, tiles, more_tiles, keep, matrix, rest, basis_in)

    return pl.pallas_call(
        final_kernel,
        out_shape=jax.ShapeDtypeStruct((leaf_dev, vectors, cells), F32),
        in_specs=[VMEM] * 4,
        out_specs=VMEM,
        compiler_params=PARAMS,
        name="final",
    )(got, folded, basis_in, base)


def solution(mesh):
    split = P(("design", "leaf", "vec"), None, None)
    in_specs = (P(("design", "leaf", "vec"), "sub", None),) + (split,) * 7 + (P(("design", "leaf", "vec"), None),) * 3
    out_specs = P(("design", "leaf", "vec"), "sub", None)
    return jax.shard_map(on_device, mesh=mesh, in_specs=in_specs, out_specs=out_specs, check_vma=False)
```

```python
import functools

import jax
import jax.numpy as jnp
from jax import lax
from jax.experimental import pallas as pl
from jax.experimental.pallas import tpu as pltpu
from jax.sharding import PartitionSpec as P

F32 = jnp.float32
BF16 = jnp.bfloat16
NODE_AXES = ("leaf", "vec")
NT = (((1,), (1,)), ((), ()))
TN = (((0,), (0,)), ((), ()))
VMEM = pl.BlockSpec(memory_space=pltpu.VMEM)
HBM = pl.BlockSpec(memory_space=pltpu.HBM)
PARAMS = pltpu.CompilerParams(vmem_limit_bytes=32 << 20)


def bits_of(count):
    return count.bit_length() - 1


def reversed_bits(value, width):
    return sum(((value >> bit) & 1) << (width - 1 - bit) for bit in range(width))


def lane_half(shape):
    return lax.broadcasted_iota(jnp.int32, shape, 1) // (shape[1] // 2)


def in_hbm(x):
    return pltpu.with_memory_space_constraint(x, pltpu.HBM)


def side_by_side(stacked, rows):
    return jnp.concatenate([stacked[at : at + rows] for at in range(0, stacked.shape[0], rows)], axis=1)


def source_kernel(nodes, *refs):
    sources, (send_ref, keep_ref, adj_ref, *later), scratch = refs[:8], refs[8:14], refs[14:]
    dst_ref, out_ref, far_ref, up_ref, *sums, sems = scratch
    first = later[2].shape[0]
    sources = (*sources[:7], sources[7].at[:first])
    copies = [
        pltpu.make_async_copy(there, here, sems.at[i])
        for i, (there, here) in enumerate(zip(sources, (dst_ref, adj_ref, out_ref, far_ref, up_ref, *later)))
    ]
    for copy in copies:
        copy.start()
    leaf_dev, vectors, _ = adj_ref.shape
    rank = out_ref.shape[1]
    far_count = dst_ref.shape[1]
    pairs = leaf_dev // 2
    wide = 2 * rank
    within = bits_of(leaf_dev)
    me = lax.axis_index(NODE_AXES)
    rows = pairs * vectors
    for one in sums:
        one[...] = jnp.zeros_like(one)
    half = lane_half((vectors, wide))
    for copy in copies[:3]:
        copy.wait()
    coefs = [
        lax.dot_general(adj_ref[j], out_ref[j], NT, preferred_element_type=F32).astype(BF16) for j in range(leaf_dev)
    ]
    for copy in copies[3:5]:
        copy.wait()
    for j in range(leaf_dev):
        contrib = jnp.dot(coefs[j], far_ref[j], preferred_element_type=F32)
        for k in range(far_count):
            block = contrib[:, k // 2 * wide : (k // 2 + 1) * wide]
            target = dst_ref[j, k]
            place = ((target >> within) ^ me) * pairs + ((target & (leaf_dev - 1)) >> 1)
            place += ((target ^ k) & 1) * (nodes * pairs)
            sums[j][place] += jnp.where(half == k % 2, block, 0.0)
    node = lax.dot_general(jnp.concatenate(coefs, axis=1), up_ref[0], NT, preferred_element_type=F32).astype(BF16)
    node = jnp.concatenate([node, node], axis=1)
    send_ref[nodes // 2 * rows :] = node
    keep_ref[nodes // 2 * rows :] = node.astype(F32)
    width = bits_of(nodes)
    for r in range(nodes):
        for p in range(pairs):
            place = reversed_bits(r, width) * pairs + p
            straight = sum(one[place] for one in sums)
            turned = sum(one[nodes * pairs + place] for one in sums)
            block = straight + pltpu.roll(turned, rank, 1)
            at = (r % (nodes // 2)) * rows + p * vectors
            if r < nodes // 2:
                keep_ref[at : at + vectors] = block
            else:
                send_ref[at : at + vectors] = block.astype(BF16)
    for copy in copies[5:]:
        copy.wait()


def top_kernel(src_hbm, top_ref, down_ref, tiles_hbm, in_hbm_ref, matrix_ref, rest_ref, tiles_ref, in_ref, src_ref, by_node, sems):
    sources = (src_hbm, tiles_hbm.at[tiles_hbm.shape[0] - tiles_ref.shape[0] :], in_hbm_ref)
    copies = [
        pltpu.make_async_copy(there, here, sems.at[i]) for i, (there, here) in enumerate(zip(sources, (src_ref, tiles_ref, in_ref)))
    ]
    for copy in copies:
        copy.start()
    rank = down_ref.shape[1]
    me = lax.axis_index(NODE_AXES)
    by_node[...] = jnp.zeros_like(by_node)
    through = lax.dot_general(top_ref[0], down_ref[0], TN, preferred_element_type=F32)
    copies[0].wait()
    for k in range(src_ref.shape[1]):
        by_node[src_ref[0, k] ^ me] += through[k * rank : (k + 1) * rank]
    matrix = by_node[...].reshape(matrix_ref.shape)
    rounded = matrix.astype(BF16)
    matrix_ref[...] = rounded
    rest_ref[...] = (matrix - rounded.astype(F32)).astype(BF16)
    for copy in copies[1:]:
        copy.wait()


def fold_kernel(matrix_ref, rest_ref, in_ref, folded_ref):
    leaf_dev, rank, cells = in_ref.shape
    known = matrix_ref.shape[0] - folded_ref.shape[0]
    for j in range(leaf_dev):
        blocks = [ref[known:, j * rank : (j + 1) * rank] for ref in (matrix_ref, rest_ref)]
        total = sum(jnp.dot(block, in_ref[j], preferred_element_type=F32) for block in blocks)
        folded_ref[:, j * cells : (j + 1) * cells] = total.astype(BF16)


def near_kernel(src_hbm, adj_ref, a_ref, b_ref, tiles_ref, more_tiles_ref, kept_ref, matrix_ref, rest_ref, in_ref, base_ref, src_ref, around, sem):
    copy = pltpu.make_async_copy(src_hbm, src_ref, sem.at[0])
    copy.start()
    leaf_dev, vectors, cells = adj_ref.shape
    rank = in_ref.shape[1]
    rows = leaf_dev // 2 * vectors
    first = tiles_ref.shape[0]
    me = lax.axis_index(NODE_AXES)
    around[:leaf_dev] = adj_ref[...]
    around[leaf_dev : 2 * leaf_dev] = a_ref[...]
    around[2 * leaf_dev :] = b_ref[...]
    coefs = side_by_side(kept_ref[rows:].astype(BF16), vectors)
    down = sum(jnp.dot(coefs, ref[: coefs.shape[1]], preferred_element_type=F32) for ref in (matrix_ref, rest_ref))
    mixed = (side_by_side(kept_ref[:rows], vectors) + down).astype(BF16)
    copy.wait()
    for j in range(leaf_dev):
        total = jnp.dot(mixed[:, j * rank : (j + 1) * rank], in_ref[j], preferred_element_type=F32)
        for k in range(src_ref.shape[1]):
            source = src_ref[j, k]
            node = source // leaf_dev
            base = jnp.where(node == me, 0, jnp.where(node == (me ^ 1), leaf_dev, 2 * leaf_dev))
            block = around[base + source % leaf_dev]
            tiles, at = (tiles_ref, j) if j < first else (more_tiles_ref, j - first)
            total += jnp.dot(block, tiles[at, k * cells : (k + 1) * cells], preferred_element_type=F32)
        base_ref[j] = total


def final_kernel(got_ref, folded_ref, in_ref, base_ref, out_ref):
    leaf_dev, vectors, cells = base_ref.shape
    rank = in_ref.shape[1]
    rows = leaf_dev // 2 * vectors
    coefs = side_by_side(got_ref[rows:], vectors)
    mixed = side_by_side(got_ref[:rows], vectors)
    for j in range(leaf_dev):
        top = jnp.dot(coefs, folded_ref[:, j * cells : (j + 1) * cells], preferred_element_type=F32)
        far = jnp.dot(mixed[:, j * rank : (j + 1) * rank], in_ref[j], preferred_element_type=F32)
        out_ref[j] = base_ref[j] + (top + far)


def on_device(
    adjoint, leaf_basis_out, leaf_basis_in, transfer_up, transfer_down, far_coupling, top_coupling, near_tiles, near_src, far_dst, top_src
):
    leaf_dev, vectors, cells = adjoint.shape
    rank = leaf_basis_out.shape[1]
    wide = 2 * rank
    pairs = leaf_dev // 2
    rows = pairs * vectors
    nodes = lax.axis_size(NODE_AXES)
    steps = bits_of(nodes)

    cores = lax.axis_size("sub")

    def swapped(x, partner, flip):
        pairs = [(i * cores + c, partner(i) * cores + (cores - 1 - c if flip else c)) for i in range(nodes) for c in range(cores)]
        return lax.ppermute(x, NODE_AXES + ("sub",), pairs)

    def like(x):
        return jax.ShapeDtypeStruct(x.shape, x.dtype)

    first = leaf_dev // 2
    tiles_shape = (first,) + near_tiles.shape[1:]
    more_shape = (leaf_dev - first,) + near_tiles.shape[1:]
    send, keep, adjoint_v, top, down, tiles = pl.pallas_call(
        functools.partial(source_kernel, nodes),
        out_shape=(
            jax.ShapeDtypeStruct((nodes // 2 * rows + vectors, wide), BF16),
            jax.ShapeDtypeStruct((nodes // 2 * rows + vectors, wide), F32),
            like(adjoint),
            like(top_coupling),
            like(transfer_down),
            jax.ShapeDtypeStruct(tiles_shape, BF16),
        ),
        in_specs=[HBM] * 8,
        out_specs=(VMEM,) * 6,
        scratch_shapes=[
            pltpu.SMEM(far_dst.shape, jnp.int32),
            pltpu.VMEM(leaf_basis_out.shape, BF16),
            pltpu.VMEM(far_coupling.shape, BF16),
            pltpu.VMEM(transfer_up.shape, BF16),
            *[pltpu.VMEM((2 * nodes * pairs, vectors, wide), F32)] * leaf_dev,
            pltpu.SemaphoreType.DMA((8,)),
        ],
        compiler_params=PARAMS,
        name="source",
    )(*map(in_hbm, (far_dst, adjoint, leaf_basis_out, far_coupling, transfer_up, top_coupling, transfer_down, near_tiles)))

    matrix, rest, more_tiles, basis_in = pl.pallas_call(
        top_kernel,
        out_shape=(
            jax.ShapeDtypeStruct((nodes * rank, leaf_dev * rank), BF16),
            jax.ShapeDtypeStruct((nodes * rank, leaf_dev * rank), BF16),
            jax.ShapeDtypeStruct(more_shape, BF16),
            like(leaf_basis_in),
        ),
        in_specs=[HBM] + [VMEM] * 2 + [HBM] * 2,
        out_specs=(VMEM,) * 4,
        scratch_shapes=[
            pltpu.SMEM(top_src.shape, jnp.int32),
            pltpu.VMEM((nodes, rank, leaf_dev * rank), F32),
            pltpu.SemaphoreType.DMA((3,)),
        ],
        compiler_params=PARAMS,
        name="top",
    )(in_hbm(top_src), top, down, in_hbm(near_tiles), in_hbm(leaf_basis_in))

    inner = [(i, i + 1 if i % 2 else i - 1) for i in range(1, nodes - 1)]
    other = [(i * cores + c, j * cores + c) for i, j in inner for c in range(cores)]
    other += [(i * cores + c, i * cores + (c + 1) % cores) for i in (0, nodes - 1) for c in range(cores)]
    send, _ = lax.optimization_barrier((send, keep))
    a = swapped(lax.optimization_barrier((adjoint_v, send, keep))[0], lambda i: i ^ 1, False)

    for step in range(steps):
        flip = step in (0, 1)
        half = (nodes >> (step + 1)) * rows
        if step:
            send = jnp.concatenate([keep[half:].astype(BF16)] + coefs, axis=0)
            keep = jnp.concatenate([keep[:half]] + [coef.astype(F32) for coef in coefs], axis=0)
        if step == 1:
            b = lax.ppermute(lax.optimization_barrier((adjoint_v, send, keep))[0], NODE_AXES + ("sub",), other)
        if step == steps - 1:
            folded = pl.pallas_call(
                fold_kernel,
                out_shape=jax.ShapeDtypeStruct((nodes // 2 * rank, leaf_dev * cells), BF16),
                in_specs=[VMEM] * 3,
                out_specs=VMEM,
                compiler_params=PARAMS,
                name="fold",
            )(lax.optimization_barrier((matrix, send))[0], rest, basis_in)
        got = swapped(send, lambda i: i ^ (1 << step), flip)
        if flip:
            keep = swapped(keep, lambda i: i, True)
        if step == 0:
            got, _ = lax.optimization_barrier((got, matrix))
            coefs = [jnp.where(jnp.arange(wide) < rank, keep[half:].astype(BF16), got[half:])]
        elif step < steps - 1:
            coefs = [keep[half:].astype(BF16), got[half:]]
        if step < steps - 1:
            keep = keep[:half] + got[:half].astype(F32)

    base = pl.pallas_call(
        near_kernel,
        out_shape=jax.ShapeDtypeStruct((leaf_dev, vectors, cells), F32),
        in_specs=[HBM] + [VMEM] * 9,
        out_specs=VMEM,
        scratch_shapes=[
            pltpu.SMEM(near_src.shape, jnp.int32),
            pltpu.VMEM((3 * leaf_dev, vectors, cells), BF16),
            pltpu.SemaphoreType.DMA((1,)),
        ],
        compiler_params=PARAMS,
        name="near",
    )(in_hbm(near_src), adjoint_v, a, b, tiles, more_tiles, keep, matrix, rest, basis_in)

    return pl.pallas_call(
        final_kernel,
        out_shape=jax.ShapeDtypeStruct((leaf_dev, vectors, cells), F32),
        in_specs=[VMEM] * 4,
        out_specs=VMEM,
        compiler_params=PARAMS,
        name="final",
    )(got, folded, basis_in, base)


def solution(mesh):
    split = P(("design", "leaf", "vec"), None, None)
    in_specs = (P(("design", "leaf", "vec"), "sub", None),) + (split,) * 7 + (P(("design", "leaf", "vec"), None),) * 3
    out_specs = P(("design", "leaf", "vec"), "sub", None)
    return jax.shard_map(on_device, mesh=mesh, in_specs=in_specs, out_specs=out_specs, check_vma=False)
```

```python
import functools

import jax
import jax.numpy as jnp
from jax import lax
from jax.experimental import pallas as pl
from jax.experimental.pallas import tpu as pltpu
from jax.sharding import PartitionSpec as P

F32 = jnp.float32
BF16 = jnp.bfloat16
NODE_AXES = ("leaf", "vec")
NT = (((1,), (1,)), ((), ()))
TN = (((0,), (0,)), ((), ()))
VMEM = pl.BlockSpec(memory_space=pltpu.VMEM)
HBM = pl.BlockSpec(memory_space=pltpu.HBM)
PARAMS = pltpu.CompilerParams(vmem_limit_bytes=32 << 20)


def bits_of(count):
    return count.bit_length() - 1


def reversed_bits(value, width):
    return sum(((value >> bit) & 1) << (width - 1 - bit) for bit in range(width))


def lane_half(shape):
    return lax.broadcasted_iota(jnp.int32, shape, 1) // (shape[1] // 2)


def in_hbm(x):
    return pltpu.with_memory_space_constraint(x, pltpu.HBM)


def side_by_side(stacked, rows):
    return jnp.concatenate([stacked[at : at + rows] for at in range(0, stacked.shape[0], rows)], axis=1)


def source_kernel(nodes, *refs):
    sources, (send_ref, keep_ref, adj_ref, *later), scratch = refs[:8], refs[8:14], refs[14:]
    dst_ref, out_ref, far_ref, up_ref, *sums, sems = scratch
    first = later[2].shape[0]
    sources = (*sources[:7], sources[7].at[:first])
    copies = [
        pltpu.make_async_copy(there, here, sems.at[i])
        for i, (there, here) in enumerate(zip(sources, (dst_ref, adj_ref, out_ref, far_ref, up_ref, *later)))
    ]
    for copy in copies:
        copy.start()
    leaf_dev, vectors, _ = adj_ref.shape
    rank = out_ref.shape[1]
    far_count = dst_ref.shape[1]
    pairs = leaf_dev // 2
    wide = 2 * rank
    within = bits_of(leaf_dev)
    me = lax.axis_index(NODE_AXES)
    rows = pairs * vectors
    for one in sums:
        one[...] = jnp.zeros_like(one)
    half = lane_half((vectors, wide))
    for copy in copies[:3]:
        copy.wait()
    coefs = [
        lax.dot_general(adj_ref[j], out_ref[j], NT, preferred_element_type=F32).astype(BF16) for j in range(leaf_dev)
    ]
    for copy in copies[3:5]:
        copy.wait()
    contribs = [jnp.dot(coefs[j], far_ref[j], preferred_element_type=F32) for j in range(leaf_dev)]
    for k in range(far_count):
        for j in range(leaf_dev):
            block = contribs[j][:, k // 2 * wide : (k // 2 + 1) * wide]
            target = dst_ref[j, k]
            place = ((target >> within) ^ me) * pairs + ((target & (leaf_dev - 1)) >> 1)
            place += ((target ^ k) & 1) * (nodes * pairs)
            sums[j][place] += jnp.where(half == k % 2, block, 0.0)
    node = lax.dot_general(jnp.concatenate(coefs, axis=1), up_ref[0], NT, preferred_element_type=F32).astype(BF16)
    node = jnp.concatenate([node, node], axis=1)
    send_ref[nodes // 2 * rows :] = node
    keep_ref[nodes // 2 * rows :] = node.astype(F32)
    width = bits_of(nodes)
    for r in range(nodes):
        for p in range(pairs):
            place = reversed_bits(r, width) * pairs + p
            straight = sum(one[place] for one in sums)
            turned = sum(one[nodes * pairs + place] for one in sums)
            block = straight + pltpu.roll(turned, rank, 1)
            at = (r % (nodes // 2)) * rows + p * vectors
            if r < nodes // 2:
                keep_ref[at : at + vectors] = block
            else:
                send_ref[at : at + vectors] = block.astype(BF16)
    for copy in copies[5:]:
        copy.wait()


def top_kernel(src_hbm, top_ref, down_ref, tiles_hbm, in_hbm_ref, matrix_ref, rest_ref, tiles_ref, in_ref, src_ref, by_node, sems):
    sources = (src_hbm, tiles_hbm.at[tiles_hbm.shape[0] - tiles_ref.shape[0] :], in_hbm_ref)
    copies = [
        pltpu.make_async_copy(there, here, sems.at[i]) for i, (there, here) in enumerate(zip(sources, (src_ref, tiles_ref, in_ref)))
    ]
    for copy in copies:
        copy.start()
    rank = down_ref.shape[1]
    me = lax.axis_index(NODE_AXES)
    by_node[...] = jnp.zeros_like(by_node)
    through = lax.dot_general(top_ref[0], down_ref[0], TN, preferred_element_type=F32)
    copies[0].wait()
    for k in range(src_ref.shape[1]):
        by_node[src_ref[0, k] ^ me] += through[k * rank : (k + 1) * rank]
    matrix = by_node[...].reshape(matrix_ref.shape)
    rounded = matrix.astype(BF16)
    matrix_ref[...] = rounded
    rest_ref[...] = (matrix - rounded.astype(F32)).astype(BF16)
    for copy in copies[1:]:
        copy.wait()


def fold_kernel(matrix_ref, rest_ref, in_ref, folded_ref):
    leaf_dev, rank, cells = in_ref.shape
    known = matrix_ref.shape[0] - folded_ref.shape[0]
    for j in range(leaf_dev):
        blocks = [ref[known:, j * rank : (j + 1) * rank] for ref in (matrix_ref, rest_ref)]
        total = sum(jnp.dot(block, in_ref[j], preferred_element_type=F32) for block in blocks)
        folded_ref[:, j * cells : (j + 1) * cells] = total.astype(BF16)


def near_kernel(src_hbm, adj_ref, a_ref, b_ref, tiles_ref, more_tiles_ref, kept_ref, matrix_ref, rest_ref, in_ref, base_ref, src_ref, around, sem):
    copy = pltpu.make_async_copy(src_hbm, src_ref, sem.at[0])
    copy.start()
    leaf_dev, vectors, cells = adj_ref.shape
    rank = in_ref.shape[1]
    rows = leaf_dev // 2 * vectors
    first = tiles_ref.shape[0]
    me = lax.axis_index(NODE_AXES)
    around[:leaf_dev] = adj_ref[...]
    around[leaf_dev : 2 * leaf_dev] = a_ref[...]
    around[2 * leaf_dev :] = b_ref[...]
    coefs = side_by_side(kept_ref[rows:].astype(BF16), vectors)
    down = sum(jnp.dot(coefs, ref[: coefs.shape[1]], preferred_element_type=F32) for ref in (matrix_ref, rest_ref))
    mixed = (side_by_side(kept_ref[:rows], vectors) + down).astype(BF16)
    copy.wait()
    for j in range(leaf_dev):
        total = jnp.dot(mixed[:, j * rank : (j + 1) * rank], in_ref[j], preferred_element_type=F32)
        for k in range(src_ref.shape[1]):
            source = src_ref[j, k]
            node = source // leaf_dev
            base = jnp.where(node == me, 0, jnp.where(node == (me ^ 1), leaf_dev, 2 * leaf_dev))
            block = around[base + source % leaf_dev]
            tiles, at = (tiles_ref, j) if j < first else (more_tiles_ref, j - first)
            total += jnp.dot(block, tiles[at, k * cells : (k + 1) * cells], preferred_element_type=F32)
        base_ref[j] = total


def final_kernel(got_ref, folded_ref, in_ref, base_ref, out_ref):
    leaf_dev, vectors, cells = base_ref.shape
    rank = in_ref.shape[1]
    rows = leaf_dev // 2 * vectors
    coefs = side_by_side(got_ref[rows:], vectors)
    mixed = side_by_side(got_ref[:rows], vectors)
    for j in range(leaf_dev):
        top = jnp.dot(coefs, folded_ref[:, j * cells : (j + 1) * cells], preferred_element_type=F32)
        far = jnp.dot(mixed[:, j * rank : (j + 1) * rank], in_ref[j], preferred_element_type=F32)
        out_ref[j] = base_ref[j] + (top + far)


def on_device(
    adjoint, leaf_basis_out, leaf_basis_in, transfer_up, transfer_down, far_coupling, top_coupling, near_tiles, near_src, far_dst, top_src
):
    leaf_dev, vectors, cells = adjoint.shape
    rank = leaf_basis_out.shape[1]
    wide = 2 * rank
    pairs = leaf_dev // 2
    rows = pairs * vectors
    nodes = lax.axis_size(NODE_AXES)
    steps = bits_of(nodes)

    cores = lax.axis_size("sub")

    def swapped(x, partner, flip):
        pairs = [(i * cores + c, partner(i) * cores + (cores - 1 - c if flip else c)) for i in range(nodes) for c in range(cores)]
        return lax.ppermute(x, NODE_AXES + ("sub",), pairs)

    def like(x):
        return jax.ShapeDtypeStruct(x.shape, x.dtype)

    first = leaf_dev // 2
    tiles_shape = (first,) + near_tiles.shape[1:]
    more_shape = (leaf_dev - first,) + near_tiles.shape[1:]
    send, keep, adjoint_v, top, down, tiles = pl.pallas_call(
        functools.partial(source_kernel, nodes),
        out_shape=(
            jax.ShapeDtypeStruct((nodes // 2 * rows + vectors, wide), BF16),
            jax.ShapeDtypeStruct((nodes // 2 * rows + vectors, wide), F32),
            like(adjoint),
            like(top_coupling),
            like(transfer_down),
            jax.ShapeDtypeStruct(tiles_shape, BF16),
        ),
        in_specs=[HBM] * 8,
        out_specs=(VMEM,) * 6,
        scratch_shapes=[
            pltpu.SMEM(far_dst.shape, jnp.int32),
            pltpu.VMEM(leaf_basis_out.shape, BF16),
            pltpu.VMEM(far_coupling.shape, BF16),
            pltpu.VMEM(transfer_up.shape, BF16),
            *[pltpu.VMEM((2 * nodes * pairs, vectors, wide), F32)] * leaf_dev,
            pltpu.SemaphoreType.DMA((8,)),
        ],
        compiler_params=PARAMS,
        name="source",
    )(*map(in_hbm, (far_dst, adjoint, leaf_basis_out, far_coupling, transfer_up, top_coupling, transfer_down, near_tiles)))

    matrix, rest, more_tiles, basis_in = pl.pallas_call(
        top_kernel,
        out_shape=(
            jax.ShapeDtypeStruct((nodes * rank, leaf_dev * rank), BF16),
            jax.ShapeDtypeStruct((nodes * rank, leaf_dev * rank), BF16),
            jax.ShapeDtypeStruct(more_shape, BF16),
            like(leaf_basis_in),
        ),
        in_specs=[HBM] + [VMEM] * 2 + [HBM] * 2,
        out_specs=(VMEM,) * 4,
        scratch_shapes=[
            pltpu.SMEM(top_src.shape, jnp.int32),
            pltpu.VMEM((nodes, rank, leaf_dev * rank), F32),
            pltpu.SemaphoreType.DMA((3,)),
        ],
        compiler_params=PARAMS,
        name="top",
    )(in_hbm(top_src), top, down, in_hbm(near_tiles), in_hbm(leaf_basis_in))

    inner = [(i, i + 1 if i % 2 else i - 1) for i in range(1, nodes - 1)]
    other = [(i * cores + c, j * cores + c) for i, j in inner for c in range(cores)]
    other += [(i * cores + c, i * cores + (c + 1) % cores) for i in (0, nodes - 1) for c in range(cores)]
    send, _ = lax.optimization_barrier((send, keep))
    a = swapped(lax.optimization_barrier((adjoint_v, send, keep))[0], lambda i: i ^ 1, False)

    for step in range(steps):
        flip = step in (0, 1)
        half = (nodes >> (step + 1)) * rows
        if step:
            send = jnp.concatenate([keep[half:].astype(BF16)] + coefs, axis=0)
            keep = jnp.concatenate([keep[:half]] + [coef.astype(F32) for coef in coefs], axis=0)
        if step == 1:
            b = lax.ppermute(lax.optimization_barrier((adjoint_v, send, keep))[0], NODE_AXES + ("sub",), other)
        if step == steps - 1:
            folded = pl.pallas_call(
                fold_kernel,
                out_shape=jax.ShapeDtypeStruct((nodes // 2 * rank, leaf_dev * cells), BF16),
                in_specs=[VMEM] * 3,
                out_specs=VMEM,
                compiler_params=PARAMS,
                name="fold",
            )(lax.optimization_barrier((matrix, send))[0], rest, basis_in)
        got = swapped(send, lambda i: i ^ (1 << step), flip)
        if flip:
            keep = swapped(keep, lambda i: i, True)
        if step == 0:
            got, _ = lax.optimization_barrier((got, matrix))
            coefs = [jnp.where(jnp.arange(wide) < rank, keep[half:].astype(BF16), got[half:])]
        elif step < steps - 1:
            coefs = [keep[half:].astype(BF16), got[half:]]
        if step < steps - 1:
            keep = keep[:half] + got[:half].astype(F32)

    base = pl.pallas_call(
        near_kernel,
        out_shape=jax.ShapeDtypeStruct((leaf_dev, vectors, cells), F32),
        in_specs=[HBM] + [VMEM] * 9,
        out_specs=VMEM,
        scratch_shapes=[
            pltpu.SMEM(near_src.shape, jnp.int32),
            pltpu.VMEM((3 * leaf_dev, vectors, cells), BF16),
            pltpu.SemaphoreType.DMA((1,)),
        ],
        compiler_params=PARAMS,
        name="near",
    )(in_hbm(near_src), adjoint_v, a, b, tiles, more_tiles, keep, matrix, rest, basis_in)

    return pl.pallas_call(
        final_kernel,
        out_shape=jax.ShapeDtypeStruct((leaf_dev, vectors, cells), F32),
        in_specs=[VMEM] * 4,
        out_specs=VMEM,
        compiler_params=PARAMS,
        name="final",
    )(got, folded, basis_in, base)


def solution(mesh):
    split = P(("design", "leaf", "vec"), None, None)
    in_specs = (P(("design", "leaf", "vec"), "sub", None),) + (split,) * 7 + (P(("design", "leaf", "vec"), None),) * 3
    out_specs = P(("design", "leaf", "vec"), "sub", None)
    return jax.shard_map(on_device, mesh=mesh, in_specs=in_specs, out_specs=out_specs, check_vma=False)
```

```python
import functools

import jax
import jax.numpy as jnp
from jax import lax
from jax.experimental import pallas as pl
from jax.experimental.pallas import tpu as pltpu
from jax.sharding import PartitionSpec as P

F32 = jnp.float32
BF16 = jnp.bfloat16
NODE_AXES = ("leaf", "vec")
NT = (((1,), (1,)), ((), ()))
TN = (((0,), (0,)), ((), ()))
VMEM = pl.BlockSpec(memory_space=pltpu.VMEM)
HBM = pl.BlockSpec(memory_space=pltpu.HBM)
PARAMS = pltpu.CompilerParams(vmem_limit_bytes=32 << 20)


def bits_of(count):
    return count.bit_length() - 1


def reversed_bits(value, width):
    return sum(((value >> bit) & 1) << (width - 1 - bit) for bit in range(width))


def lane_half(shape):
    return lax.broadcasted_iota(jnp.int32, shape, 1) // (shape[1] // 2)


def in_hbm(x):
    return pltpu.with_memory_space_constraint(x, pltpu.HBM)


def side_by_side(stacked, rows):
    return jnp.concatenate([stacked[at : at + rows] for at in range(0, stacked.shape[0], rows)], axis=1)


def source_kernel(nodes, *refs):
    sources, (send_ref, keep_ref, adj_ref, *later), scratch = refs[:8], refs[8:14], refs[14:]
    dst_ref, out_ref, far_ref, up_ref, *sums, sems = scratch
    first = later[2].shape[0]
    sources = (*sources[:7], sources[7].at[:first])
    copies = [
        pltpu.make_async_copy(there, here, sems.at[i])
        for i, (there, here) in enumerate(zip(sources, (dst_ref, adj_ref, out_ref, far_ref, up_ref, *later)))
    ]
    for copy in copies:
        copy.start()
    leaf_dev, vectors, _ = adj_ref.shape
    rank = out_ref.shape[1]
    far_count = dst_ref.shape[1]
    pairs = leaf_dev // 2
    wide = 2 * rank
    within = bits_of(leaf_dev)
    me = lax.axis_index(NODE_AXES)
    rows = pairs * vectors
    for one in sums:
        one[...] = jnp.zeros_like(one)
    half = lane_half((vectors, wide))
    for copy in copies[:3]:
        copy.wait()
    coefs = [
        lax.dot_general(adj_ref[j], out_ref[j], NT, preferred_element_type=F32).astype(BF16) for j in range(leaf_dev)
    ]
    for copy in copies[3:5]:
        copy.wait()
    for j in range(leaf_dev):
        contrib = jnp.dot(coefs[j], far_ref[j], preferred_element_type=F32)
        for k in range(far_count):
            block = contrib[:, k // 2 * wide : (k // 2 + 1) * wide]
            target = dst_ref[j, k]
            place = ((target >> within) ^ me) * pairs + ((target & (leaf_dev - 1)) >> 1)
            place += ((target ^ k) & 1) * (nodes * pairs)
            sums[j][place] += jnp.where(half == k % 2, block, 0.0)
    node = lax.dot_general(jnp.concatenate(coefs, axis=1), up_ref[0], NT, preferred_element_type=F32).astype(BF16)
    node = jnp.concatenate([node, node], axis=1)
    send_ref[nodes // 2 * rows :] = node
    keep_ref[nodes // 2 * rows :] = node.astype(F32)
    width = bits_of(nodes)
    for r in range(nodes):
        for p in range(pairs):
            place = reversed_bits(r, width) * pairs + p
            straight = sum(one[place] for one in sums)
            turned = sum(one[nodes * pairs + place] for one in sums)
            block = straight + pltpu.roll(turned, rank, 1)
            at = (r % (nodes // 2)) * rows + p * vectors
            if r < nodes // 2:
                keep_ref[at : at + vectors] = block
            else:
                send_ref[at : at + vectors] = block.astype(BF16)
    for copy in copies[5:]:
        copy.wait()


def top_kernel(src_hbm, top_ref, down_ref, tiles_hbm, in_hbm_ref, matrix_ref, rest_ref, tiles_ref, in_ref, src_ref, by_node, sems):
    sources = (src_hbm, tiles_hbm.at[tiles_hbm.shape[0] - tiles_ref.shape[0] :], in_hbm_ref)
    copies = [
        pltpu.make_async_copy(there, here, sems.at[i]) for i, (there, here) in enumerate(zip(sources, (src_ref, tiles_ref, in_ref)))
    ]
    for copy in copies:
        copy.start()
    rank = down_ref.shape[1]
    me = lax.axis_index(NODE_AXES)
    by_node[...] = jnp.zeros_like(by_node)
    through = lax.dot_general(top_ref[0], down_ref[0], TN, preferred_element_type=F32)
    copies[0].wait()
    for k in range(src_ref.shape[1]):
        by_node[src_ref[0, k] ^ me] += through[k * rank : (k + 1) * rank]
    matrix = by_node[...].reshape(matrix_ref.shape)
    rounded = matrix.astype(BF16)
    matrix_ref[...] = rounded
    rest_ref[...] = (matrix - rounded.astype(F32)).astype(BF16)
    for copy in copies[1:]:
        copy.wait()


def fold_kernel(matrix_ref, rest_ref, in_ref, folded_ref):
    leaf_dev, rank, cells = in_ref.shape
    known = matrix_ref.shape[0] - folded_ref.shape[0]
    for j in range(leaf_dev):
        blocks = [ref[known:, j * rank : (j + 1) * rank] for ref in (matrix_ref, rest_ref)]
        total = sum(jnp.dot(block, in_ref[j], preferred_element_type=F32) for block in blocks)
        folded_ref[:, j * cells : (j + 1) * cells] = total.astype(BF16)


def near_kernel(src_hbm, adj_ref, a_ref, b_ref, tiles_ref, more_tiles_ref, kept_ref, matrix_ref, rest_ref, in_ref, base_ref, src_ref, around, sem):
    copy = pltpu.make_async_copy(src_hbm, src_ref, sem.at[0])
    copy.start()
    leaf_dev, vectors, cells = adj_ref.shape
    rank = in_ref.shape[1]
    rows = leaf_dev // 2 * vectors
    first = tiles_ref.shape[0]
    me = lax.axis_index(NODE_AXES)
    around[:leaf_dev] = adj_ref[...]
    around[leaf_dev : 2 * leaf_dev] = a_ref[...]
    around[2 * leaf_dev :] = b_ref[...]
    coefs = side_by_side(kept_ref[rows:].astype(BF16), vectors)
    down = sum(jnp.dot(coefs, ref[: coefs.shape[1]], preferred_element_type=F32) for ref in (matrix_ref, rest_ref))
    mixed = (side_by_side(kept_ref[:rows], vectors) + down).astype(BF16)
    copy.wait()
    for j in range(leaf_dev):
        total = jnp.dot(mixed[:, j * rank : (j + 1) * rank], in_ref[j], preferred_element_type=F32)
        for k in range(src_ref.shape[1]):
            source = src_ref[j, k]
            node = source // leaf_dev
            base = jnp.where(node == me, 0, jnp.where(node == (me ^ 1), leaf_dev, 2 * leaf_dev))
            block = around[base + source % leaf_dev]
            tiles, at = (tiles_ref, j) if j < first else (more_tiles_ref, j - first)
            total += jnp.dot(block, tiles[at, k * cells : (k + 1) * cells], preferred_element_type=F32)
        base_ref[j] = total


def final_kernel(got_ref, folded_ref, in_ref, base_ref, out_ref):
    leaf_dev, vectors, cells = base_ref.shape
    rank = in_ref.shape[1]
    rows = leaf_dev // 2 * vectors
    coefs = side_by_side(got_ref[rows:], vectors)
    mixed = side_by_side(got_ref[:rows], vectors)
    top = jnp.dot(coefs, folded_ref[...], preferred_element_type=F32)
    for j in range(leaf_dev):
        far = jnp.dot(mixed[:, j * rank : (j + 1) * rank], in_ref[j], preferred_element_type=F32)
        out_ref[j] = base_ref[j] + (top[:, j * cells : (j + 1) * cells] + far)


def on_device(
    adjoint, leaf_basis_out, leaf_basis_in, transfer_up, transfer_down, far_coupling, top_coupling, near_tiles, near_src, far_dst, top_src
):
    leaf_dev, vectors, cells = adjoint.shape
    rank = leaf_basis_out.shape[1]
    wide = 2 * rank
    pairs = leaf_dev // 2
    rows = pairs * vectors
    nodes = lax.axis_size(NODE_AXES)
    steps = bits_of(nodes)

    cores = lax.axis_size("sub")

    def swapped(x, partner, flip):
        pairs = [(i * cores + c, partner(i) * cores + (cores - 1 - c if flip else c)) for i in range(nodes) for c in range(cores)]
        return lax.ppermute(x, NODE_AXES + ("sub",), pairs)

    def like(x):
        return jax.ShapeDtypeStruct(x.shape, x.dtype)

    first = leaf_dev // 2
    tiles_shape = (first,) + near_tiles.shape[1:]
    more_shape = (leaf_dev - first,) + near_tiles.shape[1:]
    send, keep, adjoint_v, top, down, tiles = pl.pallas_call(
        functools.partial(source_kernel, nodes),
        out_shape=(
            jax.ShapeDtypeStruct((nodes // 2 * rows + vectors, wide), BF16),
            jax.ShapeDtypeStruct((nodes // 2 * rows + vectors, wide), F32),
            like(adjoint),
            like(top_coupling),
            like(transfer_down),
            jax.ShapeDtypeStruct(tiles_shape, BF16),
        ),
        in_specs=[HBM] * 8,
        out_specs=(VMEM,) * 6,
        scratch_shapes=[
            pltpu.SMEM(far_dst.shape, jnp.int32),
            pltpu.VMEM(leaf_basis_out.shape, BF16),
            pltpu.VMEM(far_coupling.shape, BF16),
            pltpu.VMEM(transfer_up.shape, BF16),
            *[pltpu.VMEM((2 * nodes * pairs, vectors, wide), F32)] * leaf_dev,
            pltpu.SemaphoreType.DMA((8,)),
        ],
        compiler_params=PARAMS,
        name="source",
    )(*map(in_hbm, (far_dst, adjoint, leaf_basis_out, far_coupling, transfer_up, top_coupling, transfer_down, near_tiles)))

    matrix, rest, more_tiles, basis_in = pl.pallas_call(
        top_kernel,
        out_shape=(
            jax.ShapeDtypeStruct((nodes * rank, leaf_dev * rank), BF16),
            jax.ShapeDtypeStruct((nodes * rank, leaf_dev * rank), BF16),
            jax.ShapeDtypeStruct(more_shape, BF16),
            like(leaf_basis_in),
        ),
        in_specs=[HBM] + [VMEM] * 2 + [HBM] * 2,
        out_specs=(VMEM,) * 4,
        scratch_shapes=[
            pltpu.SMEM(top_src.shape, jnp.int32),
            pltpu.VMEM((nodes, rank, leaf_dev * rank), F32),
            pltpu.SemaphoreType.DMA((3,)),
        ],
        compiler_params=PARAMS,
        name="top",
    )(in_hbm(top_src), top, down, in_hbm(near_tiles), in_hbm(leaf_basis_in))

    inner = [(i, i + 1 if i % 2 else i - 1) for i in range(1, nodes - 1)]
    other = [(i * cores + c, j * cores + c) for i, j in inner for c in range(cores)]
    other += [(i * cores + c, i * cores + (c + 1) % cores) for i in (0, nodes - 1) for c in range(cores)]
    send, _ = lax.optimization_barrier((send, keep))
    a = swapped(lax.optimization_barrier((adjoint_v, send, keep))[0], lambda i: i ^ 1, False)

    for step in range(steps):
        flip = step in (0, 1)
        half = (nodes >> (step + 1)) * rows
        if step:
            send = jnp.concatenate([keep[half:].astype(BF16)] + coefs, axis=0)
            keep = jnp.concatenate([keep[:half]] + [coef.astype(F32) for coef in coefs], axis=0)
        if step == 1:
            b = lax.ppermute(lax.optimization_barrier((adjoint_v, send, keep))[0], NODE_AXES + ("sub",), other)
        if step == steps - 1:
            folded = pl.pallas_call(
                fold_kernel,
                out_shape=jax.ShapeDtypeStruct((nodes // 2 * rank, leaf_dev * cells), BF16),
                in_specs=[VMEM] * 3,
                out_specs=VMEM,
                compiler_params=PARAMS,
                name="fold",
            )(lax.optimization_barrier((matrix, send))[0], rest, basis_in)
        got = swapped(send, lambda i: i ^ (1 << step), flip)
        if flip:
            keep = swapped(keep, lambda i: i, True)
        if step == 0:
            got, _ = lax.optimization_barrier((got, matrix))
            coefs = [jnp.where(jnp.arange(wide) < rank, keep[half:].astype(BF16), got[half:])]
        elif step < steps - 1:
            coefs = [keep[half:].astype(BF16), got[half:]]
        if step < steps - 1:
            keep = keep[:half] + got[:half].astype(F32)

    base = pl.pallas_call(
        near_kernel,
        out_shape=jax.ShapeDtypeStruct((leaf_dev, vectors, cells), F32),
        in_specs=[HBM] + [VMEM] * 9,
        out_specs=VMEM,
        scratch_shapes=[
            pltpu.SMEM(near_src.shape, jnp.int32),
            pltpu.VMEM((3 * leaf_dev, vectors, cells), BF16),
            pltpu.SemaphoreType.DMA((1,)),
        ],
        compiler_params=PARAMS,
        name="near",
    )(in_hbm(near_src), adjoint_v, a, b, tiles, more_tiles, keep, matrix, rest, basis_in)

    return pl.pallas_call(
        final_kernel,
        out_shape=jax.ShapeDtypeStruct((leaf_dev, vectors, cells), F32),
        in_specs=[VMEM] * 4,
        out_specs=VMEM,
        compiler_params=PARAMS,
        name="final",
    )(got, folded, basis_in, base)


def solution(mesh):
    split = P(("design", "leaf", "vec"), None, None)
    in_specs = (P(("design", "leaf", "vec"), "sub", None),) + (split,) * 7 + (P(("design", "leaf", "vec"), None),) * 3
    out_specs = P(("design", "leaf", "vec"), "sub", None)
    return jax.shard_map(on_device, mesh=mesh, in_specs=in_specs, out_specs=out_specs, check_vma=False)
```

```python
import functools

import jax
import jax.numpy as jnp
from jax import lax
from jax.experimental import pallas as pl
from jax.experimental.pallas import tpu as pltpu
from jax.sharding import PartitionSpec as P

F32 = jnp.float32
BF16 = jnp.bfloat16
NODE_AXES = ("leaf", "vec")
NT = (((1,), (1,)), ((), ()))
TN = (((0,), (0,)), ((), ()))
VMEM = pl.BlockSpec(memory_space=pltpu.VMEM)
HBM = pl.BlockSpec(memory_space=pltpu.HBM)
PARAMS = pltpu.CompilerParams(vmem_limit_bytes=32 << 20)


def bits_of(count):
    return count.bit_length() - 1


def reversed_bits(value, width):
    return sum(((value >> bit) & 1) << (width - 1 - bit) for bit in range(width))


def lane_half(shape):
    return lax.broadcasted_iota(jnp.int32, shape, 1) // (shape[1] // 2)


def in_hbm(x):
    return pltpu.with_memory_space_constraint(x, pltpu.HBM)


def side_by_side(stacked, rows):
    return jnp.concatenate([stacked[at : at + rows] for at in range(0, stacked.shape[0], rows)], axis=1)


def source_kernel(nodes, *refs):
    sources, (send_ref, keep_ref, adj_ref, *later), scratch = refs[:8], refs[8:14], refs[14:]
    dst_ref, out_ref, far_ref, up_ref, *sums, sems = scratch
    first = later[2].shape[0]
    sources = (*sources[:7], sources[7].at[:first])
    copies = [
        pltpu.make_async_copy(there, here, sems.at[i])
        for i, (there, here) in enumerate(zip(sources, (dst_ref, adj_ref, out_ref, far_ref, up_ref, *later)))
    ]
    for copy in copies:
        copy.start()
    leaf_dev, vectors, _ = adj_ref.shape
    rank = out_ref.shape[1]
    far_count = dst_ref.shape[1]
    pairs = leaf_dev // 2
    wide = 2 * rank
    within = bits_of(leaf_dev)
    me = lax.axis_index(NODE_AXES)
    rows = pairs * vectors
    for one in sums:
        one[...] = jnp.zeros_like(one)
    half = lane_half((vectors, wide))
    for copy in copies[:3]:
        copy.wait()
    coefs = [
        lax.dot_general(adj_ref[j], out_ref[j], NT, preferred_element_type=F32).astype(BF16) for j in range(leaf_dev)
    ]
    for copy in copies[3:5]:
        copy.wait()
    for j in range(leaf_dev):
        contrib = jnp.dot(coefs[j], far_ref[j], preferred_element_type=F32)
        for k in range(far_count):
            block = contrib[:, k // 2 * wide : (k // 2 + 1) * wide]
            target = dst_ref[j, k]
            place = ((target >> within) ^ me) * pairs + ((target & (leaf_dev - 1)) >> 1)
            place += ((target ^ k) & 1) * (nodes * pairs)
            sums[j][place] += jnp.where(half == k % 2, block, 0.0)
    node = lax.dot_general(jnp.concatenate(coefs, axis=1), up_ref[0], NT, preferred_element_type=F32).astype(BF16)
    node = jnp.concatenate([node, node], axis=1)
    send_ref[nodes // 2 * rows :] = node
    keep_ref[nodes // 2 * rows :] = node.astype(F32)
    width = bits_of(nodes)
    for r in range(nodes):
        for p in range(pairs):
            place = reversed_bits(r, width) * pairs + p
            straight = sum(one[place] for one in sums)
            turned = sum(one[nodes * pairs + place] for one in sums)
            block = straight + pltpu.roll(turned, rank, 1)
            at = (r % (nodes // 2)) * rows + p * vectors
            if r < nodes // 2:
                keep_ref[at : at + vectors] = block
            else:
                send_ref[at : at + vectors] = block.astype(BF16)
    for copy in copies[5:]:
        copy.wait()


def top_kernel(src_hbm, top_ref, down_ref, tiles_hbm, in_hbm_ref, matrix_ref, rest_ref, tiles_ref, in_ref, src_ref, by_node, sems):
    sources = (src_hbm, tiles_hbm.at[tiles_hbm.shape[0] - tiles_ref.shape[0] :], in_hbm_ref)
    copies = [
        pltpu.make_async_copy(there, here, sems.at[i]) for i, (there, here) in enumerate(zip(sources, (src_ref, tiles_ref, in_ref)))
    ]
    for copy in copies:
        copy.start()
    rank = down_ref.shape[1]
    me = lax.axis_index(NODE_AXES)
    by_node[...] = jnp.zeros_like(by_node)
    through = lax.dot_general(top_ref[0], down_ref[0], TN, preferred_element_type=F32)
    copies[0].wait()
    for k in range(src_ref.shape[1]):
        by_node[src_ref[0, k] ^ me] += through[k * rank : (k + 1) * rank]
    matrix = by_node[...].reshape(matrix_ref.shape)
    rounded = matrix.astype(BF16)
    matrix_ref[...] = rounded
    rest_ref[...] = (matrix - rounded.astype(F32)).astype(BF16)
    for copy in copies[1:]:
        copy.wait()


def fold_kernel(matrix_ref, rest_ref, in_ref, folded_ref):
    leaf_dev, rank, cells = in_ref.shape
    known = matrix_ref.shape[0] - folded_ref.shape[0]
    for j in range(leaf_dev):
        blocks = [ref[known:, j * rank : (j + 1) * rank] for ref in (matrix_ref, rest_ref)]
        total = sum(jnp.dot(block, in_ref[j], preferred_element_type=F32) for block in blocks)
        folded_ref[:, j * cells : (j + 1) * cells] = total.astype(BF16)


def near_kernel(src_hbm, adj_ref, a_ref, b_ref, tiles_ref, more_tiles_ref, kept_ref, matrix_ref, rest_ref, in_ref, base_ref, src_ref, around, sem):
    copy = pltpu.make_async_copy(src_hbm, src_ref, sem.at[0])
    copy.start()
    leaf_dev, vectors, cells = adj_ref.shape
    rank = in_ref.shape[1]
    rows = leaf_dev // 2 * vectors
    first = tiles_ref.shape[0]
    me = lax.axis_index(NODE_AXES)
    around[:leaf_dev] = adj_ref[...]
    around[leaf_dev : 2 * leaf_dev] = a_ref[...]
    around[2 * leaf_dev :] = b_ref[...]
    coefs = side_by_side(kept_ref[rows:].astype(BF16), vectors)
    down = sum(jnp.dot(coefs, ref[: coefs.shape[1]], preferred_element_type=F32) for ref in (matrix_ref, rest_ref))
    mixed = (side_by_side(kept_ref[:rows], vectors) + down).astype(BF16)
    copy.wait()
    for j in range(leaf_dev):
        total = jnp.dot(mixed[:, j * rank : (j + 1) * rank], in_ref[j], preferred_element_type=F32)
        for k in range(src_ref.shape[1]):
            source = src_ref[j, k]
            node = source // leaf_dev
            base = jnp.where(node == me, 0, jnp.where(node == (me ^ 1), leaf_dev, 2 * leaf_dev))
            block = around[base + source % leaf_dev]
            tiles, at = (tiles_ref, j) if j < first else (more_tiles_ref, j - first)
            total += jnp.dot(block, tiles[at, k * cells : (k + 1) * cells], preferred_element_type=F32)
        base_ref[j] = total


def final_kernel(got_ref, folded_ref, in_ref, base_ref, out_hbm, out_ref, sems):
    leaf_dev, vectors, cells = base_ref.shape
    rank = in_ref.shape[1]
    rows = leaf_dev // 2 * vectors
    coefs = side_by_side(got_ref[rows:], vectors)
    mixed = side_by_side(got_ref[:rows], vectors)
    copies, half = [], leaf_dev // 2
    top = jnp.dot(coefs, folded_ref[...], preferred_element_type=F32)
    for j in range(leaf_dev):
        far = jnp.dot(mixed[:, j * rank : (j + 1) * rank], in_ref[j], preferred_element_type=F32)
        out_ref[j] = base_ref[j] + (top[:, j * cells : (j + 1) * cells] + far)
        if j % half == half - 1:
            part = slice(j + 1 - half, j + 1)
            copies.append(pltpu.make_async_copy(out_ref.at[part], out_hbm.at[part], sems.at[j // half]))
            copies[-1].start()
    for copy in copies:
        copy.wait()


def on_device(
    adjoint, leaf_basis_out, leaf_basis_in, transfer_up, transfer_down, far_coupling, top_coupling, near_tiles, near_src, far_dst, top_src
):
    leaf_dev, vectors, cells = adjoint.shape
    rank = leaf_basis_out.shape[1]
    wide = 2 * rank
    pairs = leaf_dev // 2
    rows = pairs * vectors
    nodes = lax.axis_size(NODE_AXES)
    steps = bits_of(nodes)

    cores = lax.axis_size("sub")

    def swapped(x, partner, flip):
        pairs = [(i * cores + c, partner(i) * cores + (cores - 1 - c if flip else c)) for i in range(nodes) for c in range(cores)]
        return lax.ppermute(x, NODE_AXES + ("sub",), pairs)

    def like(x):
        return jax.ShapeDtypeStruct(x.shape, x.dtype)

    first = leaf_dev // 2
    tiles_shape = (first,) + near_tiles.shape[1:]
    more_shape = (leaf_dev - first,) + near_tiles.shape[1:]
    send, keep, adjoint_v, top, down, tiles = pl.pallas_call(
        functools.partial(source_kernel, nodes),
        out_shape=(
            jax.ShapeDtypeStruct((nodes // 2 * rows + vectors, wide), BF16),
            jax.ShapeDtypeStruct((nodes // 2 * rows + vectors, wide), F32),
            like(adjoint),
            like(top_coupling),
            like(transfer_down),
            jax.ShapeDtypeStruct(tiles_shape, BF16),
        ),
        in_specs=[HBM] * 8,
        out_specs=(VMEM,) * 6,
        scratch_shapes=[
            pltpu.SMEM(far_dst.shape, jnp.int32),
            pltpu.VMEM(leaf_basis_out.shape, BF16),
            pltpu.VMEM(far_coupling.shape, BF16),
            pltpu.VMEM(transfer_up.shape, BF16),
            *[pltpu.VMEM((2 * nodes * pairs, vectors, wide), F32)] * leaf_dev,
            pltpu.SemaphoreType.DMA((8,)),
        ],
        compiler_params=PARAMS,
        name="source",
    )(*map(in_hbm, (far_dst, adjoint, leaf_basis_out, far_coupling, transfer_up, top_coupling, transfer_down, near_tiles)))

    matrix, rest, more_tiles, basis_in = pl.pallas_call(
        top_kernel,
        out_shape=(
            jax.ShapeDtypeStruct((nodes * rank, leaf_dev * rank), BF16),
            jax.ShapeDtypeStruct((nodes * rank, leaf_dev * rank), BF16),
            jax.ShapeDtypeStruct(more_shape, BF16),
            like(leaf_basis_in),
        ),
        in_specs=[HBM] + [VMEM] * 2 + [HBM] * 2,
        out_specs=(VMEM,) * 4,
        scratch_shapes=[
            pltpu.SMEM(top_src.shape, jnp.int32),
            pltpu.VMEM((nodes, rank, leaf_dev * rank), F32),
            pltpu.SemaphoreType.DMA((3,)),
        ],
        compiler_params=PARAMS,
        name="top",
    )(in_hbm(top_src), top, down, in_hbm(near_tiles), in_hbm(leaf_basis_in))

    inner = [(i, i + 1 if i % 2 else i - 1) for i in range(1, nodes - 1)]
    other = [(i * cores + c, j * cores + c) for i, j in inner for c in range(cores)]
    other += [(i * cores + c, i * cores + (c + 1) % cores) for i in (0, nodes - 1) for c in range(cores)]
    send, _ = lax.optimization_barrier((send, keep))
    a = swapped(lax.optimization_barrier((adjoint_v, send, keep))[0], lambda i: i ^ 1, False)

    for step in range(steps):
        flip = step in (0, 1)
        half = (nodes >> (step + 1)) * rows
        if step:
            send = jnp.concatenate([keep[half:].astype(BF16)] + coefs, axis=0)
            keep = jnp.concatenate([keep[:half]] + [coef.astype(F32) for coef in coefs], axis=0)
        if step == 1:
            b = lax.ppermute(lax.optimization_barrier((adjoint_v, send, keep))[0], NODE_AXES + ("sub",), other)
        if step == steps - 1:
            folded = pl.pallas_call(
                fold_kernel,
                out_shape=jax.ShapeDtypeStruct((nodes // 2 * rank, leaf_dev * cells), BF16),
                in_specs=[VMEM] * 3,
                out_specs=VMEM,
                compiler_params=PARAMS,
                name="fold",
            )(lax.optimization_barrier((matrix, send))[0], rest, basis_in)
        got = swapped(send, lambda i: i ^ (1 << step), flip)
        if flip:
            keep = swapped(keep, lambda i: i, True)
        if step == 0:
            got, _ = lax.optimization_barrier((got, matrix))
            coefs = [jnp.where(jnp.arange(wide) < rank, keep[half:].astype(BF16), got[half:])]
        elif step < steps - 1:
            coefs = [keep[half:].astype(BF16), got[half:]]
        if step < steps - 1:
            keep = keep[:half] + got[:half].astype(F32)

    base = pl.pallas_call(
        near_kernel,
        out_shape=jax.ShapeDtypeStruct((leaf_dev, vectors, cells), F32),
        in_specs=[HBM] + [VMEM] * 9,
        out_specs=VMEM,
        scratch_shapes=[
            pltpu.SMEM(near_src.shape, jnp.int32),
            pltpu.VMEM((3 * leaf_dev, vectors, cells), BF16),
            pltpu.SemaphoreType.DMA((1,)),
        ],
        compiler_params=PARAMS,
        name="near",
    )(in_hbm(near_src), adjoint_v, a, b, tiles, more_tiles, keep, matrix, rest, basis_in)

    return pl.pallas_call(
        final_kernel,
        out_shape=jax.ShapeDtypeStruct((leaf_dev, vectors, cells), F32),
        in_specs=[VMEM] * 4,
        out_specs=HBM,
        scratch_shapes=[pltpu.VMEM((leaf_dev, vectors, cells), F32), pltpu.SemaphoreType.DMA((2,))],
        compiler_params=PARAMS,
        name="final",
    )(got, folded, basis_in, base)


def solution(mesh):
    split = P(("design", "leaf", "vec"), None, None)
    in_specs = (P(("design", "leaf", "vec"), "sub", None),) + (split,) * 7 + (P(("design", "leaf", "vec"), None),) * 3
    out_specs = P(("design", "leaf", "vec"), "sub", None)
    return jax.shard_map(on_device, mesh=mesh, in_specs=in_specs, out_specs=out_specs, check_vma=False)
```
